256 devices in a mesh: group: 4 (over y), member: 64 (over x, z, core).
Axes of the slice: x: 4, y: 4, z: 8, core: 2. Of those that a mesh axis runs over, the one named last changes fastest.
Arguments:
- queries: bfloat16 [131072, 4096], P(('group', 'member')), may hold values from -16 to 16
- passages: bfloat16 [16384, 4096], P(('group', 'member')), may hold values from -8 to 8
- pair_blocks: int32 [256, 63, 2], replicated, may hold values from 0 to 7, as said below
- positive: int32 [131072], P(('group', 'member')), may hold values from 0 to 63
Outputs:
- loss: float32 [], replicated
- query_grad: bfloat16 [131072, 4096], P(('group', 'member'))
- passage_grad: bfloat16 [16384, 4096], P(('group', 'member'))
The draws below stay inside these ranges and needn't reach their ends.
Inputs may be any that keep to these rules, and one draw needn't show every extreme that they name: `pair_blocks`: the 2 numbers of one query block and offset are different.
All inputs are finite; a program needn't handle non-finite values.
Results may differ from the reference program's by a relative error of at most 0.007.
Values may be sent and summed in bfloat16 or wider, within the bound.
No kernel may reach another device: no remote copies, remote signals or barrier semaphores. Data moves between devices by JAX's collectives and lax.ppermute only.
A program may use at most 128 MiB of HBM per device.

```python
import jax
import jax.numpy as jnp
from jax import lax

D = 4096
TQ_DEV = 512
PASSAGE_BLOCKS_PER = 8
BR = 8
CAP = 2
TP_DEV = 64
NB = 256
NQ = 131072
NP = 16384
N_MEMBER = 64


def passage_values(key):
    values = jax.random.normal(key, (NP, D), jnp.float32)
    noise = jax.random.normal(jax.random.fold_in(key, 5), (NP, D), jnp.float32)
    second = (jnp.arange(NP) % TP_DEV == 1)[:, None]
    values = jnp.where(second, noise, values)
    return jnp.clip(values, -8.0, 8.0)


def block_rise(key, low, high):
    blocks = jnp.arange(NQ) // TQ_DEV
    share = blocks.astype(jnp.float32) / max(NB - 1, 1)
    factor = jnp.exp(jax.random.uniform(key, (NB,), jnp.float32, -0.9, 0.0))
    return ((low + (high - low) * share) * factor[blocks])[:, None]


def draw_passages(key, part):
    values = passage_values(key)
    return values.astype(jnp.bfloat16)


def draw_queries(key, part):
    key = jax.random.fold_in(key, 11)
    result = jnp.clip(jax.random.normal(key, (NQ, D), jnp.float32), -5.0, 5.0) * block_rise(jax.random.fold_in(key, 3), 0.5, 3.0)
    result = jnp.clip(result, -16.0, 16.0)
    return result.astype(jnp.bfloat16)


def draw_pair_blocks(key, part):
    key = jax.random.fold_in(key, 23)
    indicator_matrix = jax.random.randint(jax.random.fold_in(key, 1), (NB,), 0, PASSAGE_BLOCKS_PER)
    blocks = jnp.arange(NB)
    grp = blocks // N_MEMBER
    mem = blocks % N_MEMBER
    offsets = jnp.arange(N_MEMBER - 1)
    sender_index = grp[:, None] * N_MEMBER + (mem[:, None] + 1 + offsets[None, :]) % N_MEMBER
    resident_rows = jnp.arange(PASSAGE_BLOCKS_PER)
    baseline_score = jax.random.randint(key, (NB, N_MEMBER - 1, PASSAGE_BLOCKS_PER), 0, 1024)
    extra_margin = jnp.where(resident_rows[None, None, :] == indicator_matrix[sender_index][:, :, None], 768, 0)
    similarity_matrix = (baseline_score + extra_margin) * PASSAGE_BLOCKS_PER + resident_rows[None, None, :]
    picked = jax.lax.top_k(similarity_matrix, CAP)[1]
    return picked.astype(jnp.int32)


def plant(array, rng, smallest, high):
    index_at = [jax.random.randint(jax.random.fold_in(rng, axis), (), 0, length) for axis, length in enumerate(array.shape)]
    widest = array.shape.index(max(array.shape))
    next_to = index_at[:widest] + [(index_at[widest] + 1) % array.shape[widest]] + index_at[widest + 1:]
    return array.at[tuple(index_at)].set(smallest).at[tuple(next_to)].set(high)


def setup_inputs(seed: int = 0) -> dict:
    streams_of = jax.random.split(jax.random.key(seed), 5)
    queries = draw_queries(jax.random.fold_in(streams_of[4], 71), 0)
    passages = draw_passages(jax.random.fold_in(streams_of[4], 71), 0)
    pair_blocks = draw_pair_blocks(jax.random.fold_in(streams_of[4], 71), 0)
    positive = plant(jax.random.randint(streams_of[3], (NQ,), 0, TP_DEV), jax.random.fold_in(streams_of[3], 1), 0, TP_DEV - 1).astype(jnp.int32)
    return {"queries": queries, "passages": passages, "pair_blocks": pair_blocks, "positive": positive}


score_scale = 0.046875


def reference(queries, passages, pair_blocks, positive):
    query_blocks = queries.reshape(NB, TQ_DEV, D)
    pos_blocks = positive.reshape(NB, TQ_DEV)
    offsets = jnp.arange(N_MEMBER - 1, dtype=jnp.int32)
    within = jnp.arange(BR, dtype=jnp.int32)

    def per_block(grads, block):
        grp = block // N_MEMBER
        mem = block % N_MEMBER
        sender_index = grp * N_MEMBER + (mem + 1 + offsets) % N_MEMBER
        chosen = pair_blocks[block]
        remote_rows = (sender_index[:, None, None] * TP_DEV + chosen[:, :, None] * BR + within[None, None, :]).reshape(-1)
        own_rows = block * TP_DEV + jnp.arange(TP_DEV, dtype=jnp.int32)
        index = jnp.concatenate([own_rows.astype(jnp.int32), remote_rows.astype(jnp.int32)])
        keys = passages[index]
        rows_q = query_blocks[block]
        similarity_matrix = jnp.dot(rows_q, keys.T, preferred_element_type=jnp.float32) * score_scale
        top = jnp.max(similarity_matrix, axis=1)
        lse = top + jnp.log(jnp.sum(jnp.exp(similarity_matrix - top[:, None]), axis=1))
        hit = jax.nn.one_hot(pos_blocks[block], keys.shape[0], dtype=jnp.float32)
        pos_score = jnp.sum(similarity_matrix * hit, axis=1)
        term = jnp.sum(lse - pos_score)
        weights = (jnp.exp(similarity_matrix - lse[:, None]) - hit).astype(jnp.bfloat16)
        qgrad = jnp.dot(weights, keys, preferred_element_type=jnp.float32).astype(jnp.bfloat16)
        pgrad = jnp.dot(weights.T, rows_q, preferred_element_type=jnp.float32)
        grads = grads.at[index].add(pgrad)
        return grads, (term, qgrad)

    start = jnp.zeros((NP, D), jnp.float32)
    grads, (terms, qgrads) = lax.scan(per_block, start, jnp.arange(NB, dtype=jnp.int32))
    loss = jnp.sum(terms) / NQ
    return loss, qgrads.reshape(NQ, D), grads.astype(jnp.bfloat16)
```

```python
import jax
import jax.numpy as jnp
from jax import lax
from jax.experimental import pallas as pl
from jax.experimental.pallas import tpu as pltpu
from jax.sharding import PartitionSpec as P

BLOCKS = 8
BR = 8
CAP = 2
NX, NZ, NC = 4, 8, 2
WA = 3072
WB = 1024
WIDTH = WA + WB
score_scale = 0.046875

DZ = (0, -1, 1, -2, 2, -3, 3, 4)
RC = (0, -1, 1, 2)
OUT = (1, -1, 2)
CHUNKS = ((0,), (1, 2), (3, 4), (5, 6), (7,))
BACK = ((4, 3), (2, 1, 0))

ANY = pl.BlockSpec(memory_space=pl.ANY)
VMEM = pl.BlockSpec(memory_space=pltpu.VMEM)
SMEM = pl.BlockSpec(memory_space=pltpu.SMEM)


def member(x, z, c):
    return ((x % NX) * NZ + z % NZ) * NC + c % NC


def hop(a, dx=0, dz=0, dc=0):
    pairs = [
        (member(x, z, c), member(x + dx, z + dz, c + dc))
        for x in range(NX)
        for z in range(NZ)
        for c in range(NC)
    ]
    return lax.ppermute(a, "member", pairs)


def mine_at(q, iz, rc, p):
    return ((q * 8 + iz) * 4 + rc) * 2 + p


def out_at(t, iz, q, p):
    return 128 + ((t * 8 + iz) * 2 + q) * 2 + p


def bf16(*shape):
    return jax.ShapeDtypeStruct(shape, jnp.bfloat16)


def move(table, sources, copies, outs):
    n, m = len(copies), len(outs)

    def body(tab, *refs):
        src, dst = refs[: len(sources)], refs[len(sources) : len(sources) + m]
        mid, sem, sem_out = refs[len(sources) + m : -2], refs[-2], refs[-1]

        def at(ref, index):
            return ref.at[tuple(tab[i[0]] if isinstance(i, tuple) else i for i in index)]

        ops = [
            pltpu.make_async_copy(at(src[s], si), at(mid[d], di), sem.at[k])
            for k, (s, si, d, di) in enumerate(copies)
        ]
        for op in ops:
            op.start()
        last = []
        for d in range(m):
            for op, copy in zip(ops, copies):
                if copy[2] == d:
                    op.wait()
            last.append(pltpu.make_async_copy(mid[d], dst[d], sem_out.at[d]))
            last[-1].start()
        for op in last:
            op.wait()

    return pl.pallas_call(
        body,
        out_shape=outs,
        in_specs=[SMEM] + [ANY] * len(sources),
        out_specs=[ANY] * m,
        scratch_shapes=[pltpu.VMEM(o.shape, o.dtype) for o in outs]
        + [pltpu.SemaphoreType.DMA((n,)), pltpu.SemaphoreType.DMA((m,))],
        compiler_params=pltpu.CompilerParams(vmem_limit_bytes=32 * 2**20),
        cost_estimate=pl.CostEstimate(flops=0, bytes_accessed=2**20, transcendentals=0),
    )(table, *sources)


def pack(table, chunk, held):
    copies = []
    for t in range(3):
        for j, iz in enumerate(chunk):
            for q in range(2):
                for p in range(CAP):
                    copies.append((j, ((out_at(t, iz, q, p),),), t, (j, q, p)))
    outs = [bf16(len(chunk), 2, CAP, BR, WA)] * 3
    return move(table, held, copies, outs)


def assemble(table, chunk, held, rows, arrived):
    n = len(chunk)
    left, right = pl.ds(0, WA), pl.ds(WA, WB)
    every = slice(None)
    copies = []
    for j, iz in enumerate(chunk):
        for q in range(2):
            for rc in range(1, 4):
                copies.append((2 * n + rc - 1, (j, q), q, (j, rc, every, every, left)))
            for rc in range(4):
                for p in range(CAP):
                    at = (mine_at(q, iz, rc, p),)
                    copies.append((n + j, (rc, at), q, (j, rc, p, every, right)))
                    if rc == 0:
                        copies.append((j, (at,), q, (j, rc, p, every, left)))
    outs = [bf16(n, 4, CAP, BR, WIDTH)] * 2
    return move(table, [*held, *rows, *arrived], copies, outs)


def unpack(table, group, own, oth):
    copies, outs = [], []
    at = 0
    for ch in group:
        n = len(CHUNKS[ch])
        for rc in range(1, 4):
            for j in range(n):
                for q in range(2):
                    copies.append(
                        (q, (at + j, rc, slice(None), slice(None), pl.ds(0, WA)), len(outs), (j, q))
                    )
            outs.append(bf16(n, 2, CAP, BR, WA))
        at += n
    return move(table, [own, oth], copies, outs)


def sum_a(table, parts):
    counts = [len(ring) for *_, ring in parts]

    def body(tab, *refs):
        n = len(parts)
        outs, accs = refs[-2 * n : -n], refs[-n:]
        pos = 0
        for (iz, *_), count, out, acc in zip(parts, counts, outs, accs):
            own_ref, oth_ref, *come = refs[pos : pos + 5]
            ring = refs[pos + 5 : pos + 5 + count]
            pos += 5 + count
            if ring:
                total = ring[0][...].astype(jnp.float32)
                for r in ring[1:]:
                    total = total + r[...].astype(jnp.float32)
                acc[...] = total
            else:
                acc[...] = jnp.zeros_like(acc)
            for p in range(CAP):
                for q, ref in ((0, own_ref), (1, oth_ref)):
                    acc[tab[mine_at(q, iz, 0, p)]] += ref[0, 0, p].astype(jnp.float32)
                for t in range(3):
                    for q in range(2):
                        acc[tab[out_at(t, iz, q, p)]] += come[t][0, q, p].astype(jnp.float32)
            out[...] = acc[...].astype(out.dtype)

    tile = WA // 2
    whole = pl.BlockSpec((BLOCKS, BR, tile), lambda n: (0, 0, n))
    args, specs = [], []
    for iz, at, own, oth, j, arrived, ring in parts:
        args += [own, oth, *arrived, *ring]
        specs += [pl.BlockSpec((1, 1, CAP, BR, tile), lambda n, at=at: (at, 0, 0, 0, n))] * 2
        specs += [pl.BlockSpec((1, 2, CAP, BR, tile), lambda n, j=j: (j, 0, 0, 0, n))] * 3
        specs += [whole] * len(ring)
    return pl.pallas_call(
        body,
        grid=(2,),
        out_shape=[bf16(BLOCKS, BR, WA)] * len(parts),
        in_specs=[SMEM] + specs,
        out_specs=[whole] * len(parts),
        scratch_shapes=[pltpu.VMEM((BLOCKS, BR, tile), jnp.float32)] * len(parts),
        compiler_params=pltpu.CompilerParams(vmem_limit_bytes=32 * 2**20),
        cost_estimate=pl.CostEstimate(flops=0, bytes_accessed=2**20, transcendentals=0),
    )(table, *args)


def sum_b(table, parts):
    counts = [len(ring) for *_, ring in parts]

    def body(tab, *refs):
        n = len(parts)
        outs, accs = refs[-2 * n : -n], refs[-n:]
        pos = 0
        for (iz, *_), count, out, acc in zip(parts, counts, outs, accs):
            own_ref, oth_ref = refs[pos : pos + 2]
            ring = refs[pos + 2 : pos + 2 + count]
            pos += 2 + count
            if ring:
                total = ring[0][...].astype(jnp.float32)
                for r in ring[1:]:
                    total = total + r[...].astype(jnp.float32)
                acc[...] = total
            else:
                acc[...] = jnp.zeros_like(acc)
            for rc in range(4):
                for p in range(CAP):
                    for q, ref in ((0, own_ref), (1, oth_ref)):
                        acc[rc, tab[mine_at(q, iz, rc, p)]] += ref[0, rc, p].astype(jnp.float32)
            out[...] = acc[...].astype(out.dtype)

    tile = WB // 2
    whole = pl.BlockSpec((4, BLOCKS, BR, tile), lambda n: (0, 0, 0, n))
    args, specs = [], []
    for iz, at, own, oth, ring in parts:
        args += [own, oth, *ring]
        specs += [
            pl.BlockSpec((1, 4, CAP, BR, tile), lambda n, at=at: (at, 0, 0, 0, n + WA // tile))
        ] * 2
        specs += [whole] * len(ring)
    return pl.pallas_call(
        body,
        grid=(2,),
        out_shape=[bf16(4, BLOCKS, BR, WB)] * len(parts),
        in_specs=[SMEM] + specs,
        out_specs=[whole] * len(parts),
        scratch_shapes=[pltpu.VMEM((4, BLOCKS, BR, tile), jnp.float32)] * len(parts),
        compiler_params=pltpu.CompilerParams(vmem_limit_bytes=32 * 2**20),
        cost_estimate=pl.CostEstimate(flops=0, bytes_accessed=2**20, transcendentals=0),
    )(table, *args)


def after(x, *earlier):
    return lax.optimization_barrier((x, earlier))[0]


def tables(pair_blocks):
    me = lax.axis_index("member")
    grp = lax.axis_index("group")
    x, z, c = me // (NZ * NC), (me // NC) % NZ, me % NC
    dz = jnp.array(DZ, jnp.int32)
    rc = jnp.array(RC, jnp.int32)
    out = jnp.array(OUT, jnp.int32)
    core = jnp.stack([c, 1 - c]).astype(jnp.int32)
    mine_q = member(x, z, core)[:, None, None] + 0 * dz[None, :, None] + 0 * rc[None, None, :]
    mine_s = member(x + rc[None, None, :], z + dz[None, :, None], c) + 0 * core[:, None, None]
    out_q = member(x + out[:, None, None], z + 0 * dz[None, :, None], core[None, None, :])
    out_s = member(x, z + dz[None, :, None], c) + 0 * out[:, None, None] + 0 * core[None, None, :]
    q = jnp.concatenate([mine_q.reshape(-1), out_q.reshape(-1)])
    s = jnp.concatenate([mine_s.reshape(-1), out_s.reshape(-1)])
    offset = jnp.minimum((s - q - 1) % (NX * NZ * NC), NX * NZ * NC - 2)
    return pair_blocks[grp * (NX * NZ * NC) + q, offset].reshape(-1)


def dot(spec, a, b):
    return jnp.einsum(spec, a, b, preferred_element_type=jnp.float32)


def shards(queries, passages, pair_blocks, positive):
    rows_q = queries.shape[0]
    held = passages.shape[0]
    others = hop(queries, dc=1)
    blocks = passages.reshape(BLOCKS, BR, WIDTH)

    piece_a = blocks[:, :, :WA]
    piece_b = blocks[:, :, WA:]
    a = {0: piece_a, 1: hop(piece_a, dz=-1), -1: hop(piece_a, dz=1)}
    row = jnp.stack([piece_b, hop(piece_b, dx=1), hop(piece_b, dx=-1), hop(piece_b, dx=2)])
    b = {0: row, 1: hop(row, dz=-1), -1: hop(row, dz=1)}
    table = tables(pair_blocks)
    arrived = []
    for k, chunk in enumerate(CHUNKS):
        sent = pack(table, chunk, [a[DZ[iz]] for iz in chunk])
        arrived.append([hop(s, dx=t) for s, t in zip(sent, OUT)])
        if k == 1 or k == 2:
            a[k + 1], a[-k - 1] = hop(a[k], dz=-1), hop(a[-k], dz=1)
            next_a = (a[k + 1], a[-k - 1])
            b[k + 1] = hop(after(b[k], *next_a), dz=-1)
            b[-k - 1] = hop(after(b[-k], *next_a), dz=1)
        if k == 3:
            a[4] = hop(a[-3], dz=1)
            b[4] = hop(after(b[3], a[4]), dz=-1)
    hold = [(b[2], b[-2]), (b[3], b[-3]), (b[4],), (b[4],), (b[4],)]
    keys, scores, stats = [], [], []
    for ch, chunk in enumerate(CHUNKS):
        n = len(chunk)
        come = after(arrived[ch], *hold[ch])
        key = assemble(table, chunk, [a[DZ[iz]] for iz in chunk], [b[DZ[iz]] for iz in chunk], come)
        key = [k.reshape(n * 4 * CAP * BR, WIDTH) for k in key]
        s_own = dot("qd,pd->qp", queries, key[0]) * score_scale
        s_oth = dot("qd,pd->qp", others, key[1]) * score_scale
        if ch == 0:
            self_cols = jnp.arange(n * 4 * CAP * BR) < CAP * BR
            s_own = jnp.where(self_cols[None, :], -jnp.inf, s_own)
        keys.append(key)
        scores.append((s_own, s_oth))
        tops = [jnp.max(s, axis=1) for s in (s_own, s_oth)]
        sums = [jnp.sum(jnp.exp(s - m[:, None]), axis=1) for s, m in zip((s_own, s_oth), tops)]
        stats.append((tops, sums))
    local = dot("qd,pd->qp", queries, passages) * score_scale
    hit = (jnp.arange(held, dtype=jnp.int32)[None, :] == positive[:, None]).astype(jnp.float32)
    pos_score = jnp.sum(local * hit, axis=1)
    top_local = jnp.max(local, axis=1)
    sum_local = jnp.sum(jnp.exp(local - top_local[:, None]), axis=1)

    def merge(parts):
        top = parts[0][0]
        for m, _ in parts[1:]:
            top = jnp.maximum(top, m)
        return top, sum(l * jnp.exp(m - top) for m, l in parts)

    own = merge([(t[0], s[0]) for t, s in stats] + [(top_local, sum_local)])
    oth = merge([(t[1], s[1]) for t, s in stats])
    got = hop(jnp.stack([*own, *oth]), dc=1)
    top, total = merge([own, (got[2], got[3])])
    lse_own = top + jnp.log(total)
    top, total = merge([oth, (got[0], got[1])])
    lse_oth = top + jnp.log(total)
    terms = jnp.sum((lse_own - pos_score).reshape(-1, 128), axis=0, keepdims=True)
    terms = lax.all_gather(terms, ("group", "member"), axis=0, tiled=True)
    loss = jnp.sum(terms) / (rows_q * 256)

    w_own = [jnp.exp(s[0] - lse_own[:, None]).astype(jnp.bfloat16) for s in scores]
    w_oth = [jnp.exp(s[1] - lse_oth[:, None]).astype(jnp.bfloat16) for s in scores]
    w_local = (jnp.exp(local - lse_own[:, None]) - hit).astype(jnp.bfloat16)
    part_a, part_b = {}, {}
    sends = {}
    for group in BACK:
        n = sum(len(CHUNKS[ch]) for ch in group)
        g_own = dot("qp,qd->pd", jnp.concatenate([w_own[ch] for ch in group], 1), queries)
        g_oth = dot("qp,qd->pd", jnp.concatenate([w_oth[ch] for ch in group], 1), others)
        g_own, g_oth = (
            g.astype(jnp.bfloat16).reshape(n, 4, CAP, BR, WIDTH) for g in (g_own, g_oth)
        )
        sent = unpack(table, group, g_own, g_oth)
        at = 0
        for k, ch in enumerate(group):
            sends[ch] = sent[3 * k : 3 * k + 3]
            for j, iz in enumerate(CHUNKS[ch]):
                part_b[DZ[iz]] = (iz, at + j, g_own, g_oth)
            at += len(CHUNKS[ch])
    come = {}
    for ch in (4, 3, 2, 1, 0):
        to = sends[ch]
        if ch < 3:
            to = after(to, *come[ch + 2])
        come[ch] = [hop(to[0], dx=-1), hop(to[1], dx=1), hop(to[2], dx=2)]
        for j, iz in enumerate(CHUNKS[ch]):
            part_a[DZ[iz]] = (*part_b[DZ[iz]], j, come[ch])
    up_a, down_a, up_b, down_b = [], [], [], []
    (four,) = sum_b(table, [(*part_b[4], [])])
    down_b = [hop(four, dz=-1)]
    (four,) = sum_a(table, [(*part_a[4], [])])
    up_a = [hop(four, dz=1)]
    for k in (3, 2, 1):
        up, down = sum_b(table, [(*part_b[k], up_b), (*part_b[-k], down_b)])
        up_b, down_b = [hop(up, dz=1)], [hop(down, dz=-1)]
        up, down = sum_a(table, [(*part_a[k], up_a), (*part_a[-k], down_a)])
        up_a, down_a = [hop(up, dz=1)], [hop(down, dz=-1)]
    (all_b,) = sum_b(table, [(*part_b[0], up_b + down_b)])
    (got_a,) = sum_a(table, [(*part_a[0], up_a + down_a)])
    got_b = [all_b[0], hop(all_b[1], dx=-1), hop(all_b[2], dx=1), hop(all_b[3], dx=2)]
    got_b = sum(g.astype(jnp.float32) for g in got_b)
    got = jnp.concatenate([got_a.astype(jnp.float32), got_b], axis=2).reshape(held, WIDTH)
    own_grad = dot("qp,qd->pd", w_local, queries)
    passage_grad = (own_grad + got).astype(jnp.bfloat16)

    k_own = jnp.concatenate([k[0] for k in keys] + [passages], 0)
    k_oth = jnp.concatenate([k[1] for k in keys], 0)
    for_other = dot("qp,pd->qd", jnp.concatenate(w_oth, 1), k_oth).astype(jnp.bfloat16)
    from_other = hop(for_other, dc=1)
    query_grad = dot("qp,pd->qd", jnp.concatenate(w_own + [w_local], 1), k_own)
    query_grad = (query_grad + from_other.astype(jnp.float32)).astype(jnp.bfloat16)
    return (loss, query_grad, passage_grad)


def solution(mesh):
    in_specs = (
        P(("group", "member"), None),
        P(("group", "member"), None),
        P(),
        P(("group", "member")),
    )
    out_specs = (P(), P(("group", "member"), None), P(("group", "member"), None))
    return jax.shard_map(shards, mesh=mesh, in_specs=in_specs, out_specs=out_specs, check_vma=False)
```

```python
import jax
import jax.numpy as jnp
from jax import lax
from jax.experimental import pallas as pl
from jax.experimental.pallas import tpu as pltpu
from jax.sharding import PartitionSpec as P

BLOCKS = 8
BR = 8
CAP = 2
NX, NZ, NC = 4, 8, 2
WIDTH = 4096
COST = 1024
PASSAGES = BLOCKS * BR
score_scale = 0.046875

DZ = (0, -1, 1, -2, 2, -3, 3, 4)
TO = (0, 1, -1, 2)
CHUNKS = ((0,), (1, 2), (3, 4), (5, 6), (7,))
LOOKS = ((1, 0, 2), (3, 4))
BACK = ((3, 4), (1, 0, 2))

ANY = pl.BlockSpec(memory_space=pl.ANY)
VMEM = pl.BlockSpec(memory_space=pltpu.VMEM)
SMEM = pl.BlockSpec(memory_space=pltpu.SMEM)


def member(x, z, c):
    return ((x % NX) * NZ + z % NZ) * NC + c % NC


def hop(a, dx=0, dz=0, dc=0):
    pairs = [
        (member(x, z, c), member(x + dx, z + dz, c + dc))
        for x in range(NX)
        for z in range(NZ)
        for c in range(NC)
    ]
    return lax.ppermute(a, "member", pairs)


def pick(tab, d, q, dx, dz, p):
    last = NX * NZ * NC - 2
    base = NX * NC * (last + 1) * CAP
    x, z, c = tab[base], tab[base + 1], tab[base + 2]
    core = c if q == 0 else 1 - c
    query = (((x + d) & (NX - 1)) * NZ + z) * NC + core
    source = (((x + dx) & (NX - 1)) * NZ + ((z + dz) & (NZ - 1))) * NC + c
    offset = jnp.minimum((source - query - 1) & (last + 1), last)
    return tab[(((d % NX) * NC + core) * (last + 1) + offset) * CAP + p]


def bf16(*shape):
    return jax.ShapeDtypeStruct(shape, jnp.bfloat16)


def pack(table, chunk, held):
    n = len(chunk)
    todo = [(t, j, q, p) for t in range(4) for j in range(n) for q in range(2) for p in range(CAP)]

    def body(tab, *refs):
        src, dst, sem = refs[:n], refs[n : n + 4], refs[-1]
        ops = []
        for k, (t, j, q, p) in enumerate(todo):
            at = pick(tab, TO[t], q, 0, DZ[chunk[j]], p)
            ops.append(pltpu.make_async_copy(src[j].at[at], dst[t].at[q, j, p], sem.at[k]))
            ops[-1].start()
        for op in ops:
            op.wait()

    return pl.pallas_call(
        body,
        out_shape=[bf16(2, n, CAP, BR, WIDTH)] * 4,
        in_specs=[SMEM] + [ANY] * n,
        out_specs=[VMEM] * 4,
        scratch_shapes=[pltpu.SemaphoreType.DMA((len(todo),))],
        compiler_params=pltpu.CompilerParams(vmem_limit_bytes=32 * 2**20),
        cost_estimate=pl.CostEstimate(flops=0, bytes_accessed=COST, transcendentals=0),
    )(table, *held)


def flat(part):
    return part.reshape(2, -1, WIDTH)


def columns_of(group):
    at, places = 0, {}
    for ch in group:
        n = 4 * len(CHUNKS[ch]) * CAP * BR + (PASSAGES if ch == 0 else 0)
        places[ch] = (at, n)
        at += n
    return places, at


def score(group, keys, queries, others, passages, positive, before):
    rows = queries.shape[0]
    tile = rows // 2
    places, n = columns_of(group)
    count = 4 * len(group)

    def body(*refs):
        own, oth = refs[count : count + 2]
        more = refs[count + 2 : -3]
        out, stat, held = refs[-3:]

        @pl.when(pl.program_id(1) == 0)
        def _():
            for k, ch in enumerate(group):
                at, size = places[ch]
                for ref in refs[4 * k : 4 * k + 4]:
                    held[at : at + ref.shape[1], :] = ref[0]
                    at += ref.shape[1]
                if ch == 0:
                    held[at : at + PASSAGES, :] = more[0][...]

        lane = lax.broadcasted_iota(jnp.int32, (tile, n), 1)
        lane_out = lax.broadcasted_iota(jnp.int32, (tile, 128), 1)

        def product(ref, q):
            x = score_scale * lax.dot_general(
                ref[...], held[...], (((1,), (1,)), ((), ())), preferred_element_type=jnp.float32
            )
            if 0 in group:
                start, size = places[0]
                local = start + size - PASSAGES
                low, high = (start, start + CAP * BR) if q == 0 else (local, start + size)
                x = jnp.where((lane >= low) & (lane < high), -jnp.inf, x)
            out[0] = x
            top = jnp.max(x, axis=1, keepdims=True)
            positive_score = jnp.zeros_like(top)
            if before is not None:
                last = more[-1][0]
                rest, top = top, jnp.maximum(top, last[:, 0:1])
                positive_score = last[:, 2:3]
            total = jnp.sum(jnp.exp(x - top), axis=1, keepdims=True)
            if before is not None:
                total = total + last[:, 1:2] * jnp.exp(last[:, 0:1] - top)
            if 0 in group and q == 0:
                hit = lane == more[1][...] + local
                positive_score += jnp.sum(jnp.where(hit, x, 0.0), axis=1, keepdims=True)
            stat[0] = jnp.where(lane_out == 0, top, jnp.where(lane_out == 1, total, positive_score))

        @pl.when(pl.program_id(0) == 0)
        def _():
            product(own, 0)

        @pl.when(pl.program_id(0) == 1)
        def _():
            product(oth, 1)

    args, specs = [], []
    for ch in group:
        for part in keys[ch]:
            args.append(part)
            specs.append(pl.BlockSpec((1, part.shape[1], WIDTH), lambda q, t: (q, 0, 0)))
    args += [queries, others]
    specs += [
        pl.BlockSpec((tile, WIDTH), lambda q, t: (jnp.where(q == 0, t, 1), 0)),
        pl.BlockSpec((tile, WIDTH), lambda q, t: (jnp.where(q == 0, 0, t), 0)),
    ]
    if 0 in group:
        args += [passages, positive]
        specs.append(pl.BlockSpec((PASSAGES, WIDTH), lambda q, t: (0, 0)))
        specs.append(pl.BlockSpec((tile, 1), lambda q, t: (t, 0)))
    if before is not None:
        args.append(before)
        specs.append(pl.BlockSpec((1, tile, 128), lambda q, t: (q, t, 0)))
    return pl.pallas_call(
        body,
        grid=(2, 2),
        out_shape=[
            jax.ShapeDtypeStruct((2, rows, n), jnp.float32),
            jax.ShapeDtypeStruct((2, rows, 128), jnp.float32),
        ],
        in_specs=specs,
        out_specs=[
            pl.BlockSpec((1, tile, n), lambda q, t: (q, t, 0)),
            pl.BlockSpec((1, tile, 128), lambda q, t: (q, t, 0)),
        ],
        scratch_shapes=[pltpu.VMEM((n, WIDTH), jnp.bfloat16)],
        compiler_params=pltpu.CompilerParams(vmem_limit_bytes=56 * 2**20),
        cost_estimate=pl.CostEstimate(flops=0, bytes_accessed=COST, transcendentals=0),
    )(*args)


def log_sum(a, b):
    top = jnp.maximum(a[:, 0:1], b[:, 0:1])
    return top + jnp.log(
        a[:, 1:2] * jnp.exp(a[:, 0:1] - top) + b[:, 1:2] * jnp.exp(b[:, 0:1] - top)
    )


def partials(group, scores, column, mine, got, queries, others, positive):
    rows = queries.shape[0]
    tile = WIDTH // 4
    places, n = columns_of(group)
    sizes = [len(CHUNKS[ch]) * CAP * BR for ch in group]
    count = 4 * len(group)

    def body(s, mine_ref, got_ref, own, oth, pos, *refs):
        outs, w, turned = refs[:count], refs[count], refs[-1]

        @pl.when(pl.program_id(0) == 0)
        def _():
            for q in range(2):
                x = jnp.exp(s[q] - log_sum(mine_ref[q], got_ref[1 - q]))
                if 0 in group and q == 0:
                    lane = lax.broadcasted_iota(jnp.int32, x.shape, 1)
                    local = sum(places[0]) - PASSAGES
                    x = x - (lane == pos[...] + local).astype(jnp.float32)
                w[q] = x.astype(jnp.bfloat16)
                if n % 128:
                    x = jnp.concatenate([x, jnp.zeros((rows, 128 - n % 128), jnp.float32)], 1)
                turned[q] = x.T[:n].astype(jnp.bfloat16)

        for q, ref in enumerate((own, oth)):
            g = jnp.dot(turned[q], ref[...], preferred_element_type=jnp.float32)
            for k, (ch, m) in enumerate(zip(group, sizes)):
                at = places[ch][0]
                for r in range(4):
                    outs[4 * k + r][q] = g[at : at + m].astype(jnp.bfloat16)
                    at += m
                if ch == 0 and q == 0:
                    refs[count + 1][...] = g[at : at + PASSAGES]

    query = pl.BlockSpec((rows, tile), lambda i: (0, i))
    stat = pl.BlockSpec((2, rows, 128), lambda i: (0, 0, 0))
    outs = [m for m in sizes for _ in range(4)]
    out_shape = [bf16(2, m, WIDTH) for m in outs] + [bf16(2, rows, n)]
    out_specs = [pl.BlockSpec((2, m, tile), lambda i: (0, 0, i)) for m in outs]
    out_specs.append(pl.BlockSpec((2, rows, n), lambda i: (0, 0, 0)))
    if 0 in group:
        out_shape.append(jax.ShapeDtypeStruct((PASSAGES, WIDTH), jnp.float32))
        out_specs.append(pl.BlockSpec((PASSAGES, tile), lambda i: (0, i)))
    return pl.pallas_call(
        body,
        grid=(4,),
        out_shape=out_shape,
        in_specs=[
            pl.BlockSpec((2, rows, n), lambda i: (0, 0, column // n)),
            stat,
            stat,
            query,
            query,
            pl.BlockSpec((rows, 1), lambda i: (0, 0)),
        ],
        out_specs=out_specs,
        scratch_shapes=[pltpu.VMEM((2, n, rows), jnp.bfloat16)],
        compiler_params=pltpu.CompilerParams(vmem_limit_bytes=56 * 2**20),
        cost_estimate=pl.CostEstimate(flops=0, bytes_accessed=COST, transcendentals=0),
    )(scores, mine, got, queries, others, positive)


def query_sums(q, weights, keys, more=None):
    rows = weights[0].shape[1]
    tile = WIDTH // 4
    widths = [w.shape[2] for w in weights]

    def body(*refs):
        w_refs, parts = refs[: len(weights)], refs[len(weights) : len(weights) + len(keys)]
        out, w_all, held = refs[-3:]

        @pl.when(pl.program_id(0) == 0)
        def _():
            at = 0
            for w, n in zip(w_refs, widths):
                w_all[:, at : at + n] = w[0]
                at += n

        at = 0
        for ref in parts:
            m = ref.shape[1]
            held[at : at + m, :] = ref[0]
            at += m
        total = jnp.dot(w_all[...], held[...], preferred_element_type=jnp.float32)
        if more is not None:
            total = total + refs[len(weights) + len(keys)][...].astype(jnp.float32)
        out[...] = total.astype(out.dtype)

    specs = [pl.BlockSpec((1, rows, n), lambda i: (q, 0, 0)) for n in widths]
    for k in keys:
        last = k.shape[0] - 1
        specs.append(pl.BlockSpec((1, k.shape[1], tile), lambda i, at=min(q, last): (at, 0, i)))
    args = [*weights, *keys]
    if more is not None:
        args.append(more)
        specs.append(pl.BlockSpec((rows, tile), lambda i: (0, i)))
    return pl.pallas_call(
        body,
        grid=(4,),
        out_shape=bf16(rows, WIDTH),
        in_specs=specs,
        out_specs=pl.BlockSpec((rows, tile), lambda i: (0, i)),
        scratch_shapes=[
            pltpu.VMEM((rows, sum(widths)), jnp.bfloat16),
            pltpu.VMEM((sum(widths), tile), jnp.bfloat16),
        ],
        compiler_params=pltpu.CompilerParams(vmem_limit_bytes=56 * 2**20),
        cost_estimate=pl.CostEstimate(flops=0, bytes_accessed=COST, transcendentals=0),
    )(*args)


def add_up(table, parts):
    counts = [len(ring) for *_, ring in parts]
    tile = WIDTH // 2

    def body(tab, *refs):
        n = len(parts)
        outs, accs = refs[-2 * n : -n], refs[-n:]
        pos = 0
        for (iz, *_), count, out, acc in zip(parts, counts, outs, accs):
            row = refs[pos : pos + 4]
            ring = refs[pos + 4 : pos + 4 + count]
            pos += 4 + count
            if ring:
                total = ring[0][...].astype(jnp.float32)
                for r in ring[1:]:
                    total = total + r[...].astype(jnp.float32)
                acc[...] = total
            else:
                acc[...] = jnp.zeros_like(acc)
            for t in range(4):
                for q in range(2):
                    for p in range(CAP):
                        at = pick(tab, TO[t], q, 0, DZ[iz], p)
                        acc[at] += row[t][q, 0, p].astype(jnp.float32)
            out[...] = acc[...].astype(out.dtype)

    whole = pl.BlockSpec((BLOCKS, BR, tile), lambda n: (0, 0, n))
    args, specs = [], []
    for iz, j, row, ring in parts:
        args += [*row, *ring]
        specs += [pl.BlockSpec((2, 1, CAP, BR, tile), lambda n, j=j: (0, j, 0, 0, n))] * 4
        specs += [whole] * len(ring)
    return pl.pallas_call(
        body,
        grid=(2,),
        out_shape=[bf16(BLOCKS, BR, WIDTH)] * len(parts),
        in_specs=[SMEM] + specs,
        out_specs=[whole] * len(parts),
        scratch_shapes=[pltpu.VMEM((BLOCKS, BR, tile), jnp.float32)] * len(parts),
        compiler_params=pltpu.CompilerParams(vmem_limit_bytes=32 * 2**20),
        cost_estimate=pl.CostEstimate(flops=0, bytes_accessed=COST, transcendentals=0),
    )(table, *args)


def total_of(term):
    total = jnp.full((1, 128), term)
    for step in (1, 2):
        total = total + lax.ppermute(total, "group", [(i, i ^ step) for i in range(4)])
    total = jnp.broadcast_to(total, (NX * NZ * NC, 128))
    return jnp.sum(lax.all_to_all(total, "member", 0, 0, tiled=True)[:, 0])


def after(x, *earlier):
    if not earlier:
        return x
    return lax.optimization_barrier((x, earlier))[0]


def tables(pair_blocks):
    me = lax.axis_index("member")
    grp = lax.axis_index("group")
    x, z, c = me // (NZ * NC), (me // NC) % NZ, me % NC
    size = NX * NZ * NC
    rows = [
        lax.dynamic_slice(
            pair_blocks,
            (grp * size + member(x + d, z, 0), 0, 0),
            (NC, size - 1, CAP),
        )
        for d in range(NX)
    ]
    rows = jnp.concatenate(rows).reshape(-1)
    return jnp.concatenate([rows, jnp.stack([x, z, c]).astype(jnp.int32)])


def shards(queries, passages, pair_blocks, positive):
    rows_q = queries.shape[0]
    positive = positive.reshape(rows_q, 1)
    blocks = passages.reshape(BLOCKS, BR, WIDTH)

    a = {0: blocks, 1: hop(blocks, dz=-1), -1: hop(blocks, dz=1)}
    table = tables(pair_blocks)
    keys = []
    for k, chunk in enumerate(CHUNKS):
        if k > 1:
            gate = keys[0][1:] if k == 2 else (others,) if k == 3 else ()
            if k < 4:
                a[k] = hop(after(a[k - 1], *gate), dz=-1)
            a[-k if k < 4 else 4] = hop(after(a[-k + 1], *gate), dz=1)
        pieces = [a[DZ[iz]] for iz in chunk]
        if k == 1:
            pieces = after(pieces, *sent)
        mine, *sent = pack(table, chunk, pieces)
        going = after(sent, *keys[k - 2][1:]) if k > 1 else sent
        if k == 4:
            flat_keys = [[flat(part) for part in key] for key in keys]
            early, own = score(LOOKS[0], flat_keys, queries, others, passages, positive, None)
            going = after(going, own)
        keys.append([mine] + [hop(s, dx=t) for s, t in zip(going, TO[1:])])
        if k == 0:
            others = hop(after(queries, *keys[0][1:], a[1], a[-1]), dc=1)
    flat_keys.append([flat(part) for part in keys[4]])
    late, own = score(LOOKS[1], flat_keys, queries, others, passages, positive, own)
    got = hop(own, dc=1)

    grads, weights, come = {}, {}, {}

    def products(group, scores, column=0):
        made = partials(group, scores, column, own, got, queries, others, positive)
        for k, ch in enumerate(group):
            n = len(CHUNKS[ch])
            grads[ch] = [g.reshape(2, n, CAP, BR, WIDTH) for g in made[4 * k : 4 * k + 4]]
        weights[group] = made[4 * len(group)]
        return made[-1]

    def send(ch, *earlier):
        to = grads[ch][1:]
        if earlier:
            to = after(to, *earlier)
        come[ch] = [hop(to[1], dx=1), hop(to[0], dx=-1), hop(to[2], dx=2)]

    def row(ch):
        return [grads[ch][0], come[ch][1], come[ch][0], come[ch][2]]

    products(BACK[0], late)
    send(4)
    send(3)
    own_grad = products(BACK[1], after(early, *come[4])).reshape(BLOCKS, BR, WIDTH)
    send(2)
    send(1, *come[3])
    send(0, *come[2])
    (four,) = add_up(table, [(7, 0, row(4), [])])
    up_ring, down_ring = [hop(four, dz=1)], []
    all_keys = [*flat_keys[1], *flat_keys[0], passages[None], *flat_keys[2], *flat_keys[3], *flat_keys[4]]
    all_weights = [weights[group] for group in BACK[::-1]]
    term = jnp.sum(log_sum(own[0], got[1]) - own[0, :, 2:3])
    loss = total_of(after(term, *come[3])) / (rows_q * NX * NZ * NC * 4)
    for ch in (3, 2, 1):
        j, i = CHUNKS[ch]
        rows = row(ch)
        if ch == 1:
            for_other = query_sums(1, after(all_weights, *come[2], up, down), all_keys)
            from_other = hop(after(for_other, *come[1], *up_ring, *down_ring, loss), dc=1)
        up, down = add_up(table, [(i, 1, rows, up_ring), (j, 0, rows, down_ring)])
        up_ring, down_ring = [hop(up, dz=1)], [hop(down, dz=-1)]
    query_grad = query_sums(0, all_weights, all_keys, from_other)
    last = after(own_grad, query_grad)
    (passage_grad,) = add_up(table, [(0, 0, row(0), up_ring + down_ring + [last])])
    return (loss, query_grad, passage_grad.reshape(PASSAGES, WIDTH))


def solution(mesh):
    in_specs = (
        P(("group", "member"), None),
        P(("group", "member"), None),
        P(),
        P(("group", "member")),
    )
    out_specs = (P(), P(("group", "member"), None), P(("group", "member"), None))
    return jax.shard_map(shards, mesh=mesh, in_specs=in_specs, out_specs=out_specs, check_vma=False)
```

```python
import jax
import jax.numpy as jnp
from jax import lax
from jax.experimental import pallas as pl
from jax.experimental.pallas import tpu as pltpu
from jax.sharding import PartitionSpec as P

BLOCKS = 8
BR = 8
CAP = 2
NX, NZ, NC = 4, 8, 2
WIDTH = 4096
COST = 1024
PASSAGES = BLOCKS * BR
score_scale = 0.046875

DZ = (0, -1, 1, -2, 2, -3, 3, 4)
TO = (0, 1, -1, 2)
CHUNKS = ((0,), (1, 2), (3, 4), (5, 6), (7,))
LOOKS = ((1, 0, 2), (3, 4))
BACK = ((3, 4), (1, 0, 2))

ANY = pl.BlockSpec(memory_space=pl.ANY)
VMEM = pl.BlockSpec(memory_space=pltpu.VMEM)
SMEM = pl.BlockSpec(memory_space=pltpu.SMEM)


def member(x, z, c):
    return ((x % NX) * NZ + z % NZ) * NC + c % NC


def hop(a, dx=0, dz=0, dc=0):
    pairs = [
        (member(x, z, c), member(x + dx, z + dz, c + dc))
        for x in range(NX)
        for z in range(NZ)
        for c in range(NC)
    ]
    return lax.ppermute(a, "member", pairs)


def pick(tab, d, q, dx, dz, p):
    last = NX * NZ * NC - 2
    base = NX * NC * (last + 1) * CAP
    x, z, c = tab[base], tab[base + 1], tab[base + 2]
    core = c if q == 0 else 1 - c
    query = (((x + d) & (NX - 1)) * NZ + z) * NC + core
    source = (((x + dx) & (NX - 1)) * NZ + ((z + dz) & (NZ - 1))) * NC + c
    offset = jnp.minimum((source - query - 1) & (last + 1), last)
    return tab[(((d % NX) * NC + core) * (last + 1) + offset) * CAP + p]


def bf16(*shape):
    return jax.ShapeDtypeStruct(shape, jnp.bfloat16)


def pack(table, chunk, held):
    n = len(chunk)
    todo = [(t, j, q, p) for t in range(4) for j in range(n) for q in range(2) for p in range(CAP)]

    def body(tab, *refs):
        src, dst, sem = refs[:n], refs[n : n + 4], refs[-1]
        ops = []
        for k, (t, j, q, p) in enumerate(todo):
            at = pick(tab, TO[t], q, 0, DZ[chunk[j]], p)
            ops.append(pltpu.make_async_copy(src[j].at[at], dst[t].at[q, j, p], sem.at[k]))
            ops[-1].start()
        for op in ops:
            op.wait()

    return pl.pallas_call(
        body,
        out_shape=[bf16(2, n, CAP, BR, WIDTH)] * 4,
        in_specs=[SMEM] + [ANY] * n,
        out_specs=[VMEM] * 4,
        scratch_shapes=[pltpu.SemaphoreType.DMA((len(todo),))],
        compiler_params=pltpu.CompilerParams(vmem_limit_bytes=32 * 2**20),
        cost_estimate=pl.CostEstimate(flops=0, bytes_accessed=COST, transcendentals=0),
    )(table, *held)


def flat(part):
    return part.reshape(2, -1, WIDTH)


def columns_of(group):
    at, places = 0, {}
    for ch in group:
        n = 4 * len(CHUNKS[ch]) * CAP * BR + (PASSAGES if ch == 0 else 0)
        places[ch] = (at, n)
        at += n
    return places, at


def score(group, keys, queries, others, passages, positive, before):
    rows = queries.shape[0]
    tile = rows // 2
    places, n = columns_of(group)
    count = 4 * len(group)

    def body(*refs):
        own, oth = refs[count : count + 2]
        more = refs[count + 2 : -3]
        out, stat, held = refs[-3:]

        @pl.when(pl.program_id(1) == 0)
        def _():
            for k, ch in enumerate(group):
                at, size = places[ch]
                for ref in refs[4 * k : 4 * k + 4]:
                    held[at : at + ref.shape[1], :] = ref[0]
                    at += ref.shape[1]
                if ch == 0:
                    held[at : at + PASSAGES, :] = more[0][...]

        lane = lax.broadcasted_iota(jnp.int32, (tile, n), 1)
        lane_out = lax.broadcasted_iota(jnp.int32, (tile, 128), 1)

        def product(ref, q):
            x = score_scale * lax.dot_general(
                ref[...], held[...], (((1,), (1,)), ((), ())), preferred_element_type=jnp.float32
            )
            if 0 in group:
                start, size = places[0]
                local = start + size - PASSAGES
                low, high = (start, start + CAP * BR) if q == 0 else (local, start + size)
                x = jnp.where((lane >= low) & (lane < high), -jnp.inf, x)
            out[0] = x
            top = jnp.max(x, axis=1, keepdims=True)
            positive_score = jnp.zeros_like(top)
            if before is not None:
                last = more[-1][0]
                rest, top = top, jnp.maximum(top, last[:, 0:1])
                positive_score = last[:, 2:3]
            total = jnp.sum(jnp.exp(x - top), axis=1, keepdims=True)
            if before is not None:
                total = total + last[:, 1:2] * jnp.exp(last[:, 0:1] - top)
            if 0 in group and q == 0:
                hit = lane == more[1][...] + local
                positive_score += jnp.sum(jnp.where(hit, x, 0.0), axis=1, keepdims=True)
            stat[0] = jnp.where(lane_out == 0, top, jnp.where(lane_out == 1, total, positive_score))

        @pl.when(pl.program_id(0) == 0)
        def _():
            product(own, 0)

        @pl.when(pl.program_id(0) == 1)
        def _():
            product(oth, 1)

    args, specs = [], []
    for ch in group:
        for part in keys[ch]:
            args.append(part)
            specs.append(pl.BlockSpec((1, part.shape[1], WIDTH), lambda q, t: (q, 0, 0)))
    args += [queries, others]
    specs += [
        pl.BlockSpec((tile, WIDTH), lambda q, t: (jnp.where(q == 0, t, 1), 0)),
        pl.BlockSpec((tile, WIDTH), lambda q, t: (jnp.where(q == 0, 0, t), 0)),
    ]
    if 0 in group:
        args += [passages, positive]
        specs.append(pl.BlockSpec((PASSAGES, WIDTH), lambda q, t: (0, 0)))
        specs.append(pl.BlockSpec((tile, 1), lambda q, t: (t, 0)))
    if before is not None:
        args.append(before)
        specs.append(pl.BlockSpec((1, tile, 128), lambda q, t: (q, t, 0)))
    return pl.pallas_call(
        body,
        grid=(2, 2),
        out_shape=[
            jax.ShapeDtypeStruct((2, rows, n), jnp.float32),
            jax.ShapeDtypeStruct((2, rows, 128), jnp.float32),
        ],
        in_specs=specs,
        out_specs=[
            pl.BlockSpec((1, tile, n), lambda q, t: (q, t, 0)),
            pl.BlockSpec((1, tile, 128), lambda q, t: (q, t, 0)),
        ],
        scratch_shapes=[pltpu.VMEM((n, WIDTH), jnp.bfloat16)],
        compiler_params=pltpu.CompilerParams(vmem_limit_bytes=56 * 2**20),
        cost_estimate=pl.CostEstimate(flops=0, bytes_accessed=COST, transcendentals=0),
    )(*args)


def log_sum(a, b):
    top = jnp.maximum(a[:, 0:1], b[:, 0:1])
    return top + jnp.log(
        a[:, 1:2] * jnp.exp(a[:, 0:1] - top) + b[:, 1:2] * jnp.exp(b[:, 0:1] - top)
    )


def partials(group, scores, column, mine, got, queries, others, positive):
    rows = queries.shape[0]
    tile = WIDTH // 4
    places, n = columns_of(group)
    sizes = [len(CHUNKS[ch]) * CAP * BR for ch in group]
    count = 4 * len(group)

    def body(s, mine_ref, got_ref, own, oth, pos, *refs):
        outs, w, turned = refs[:count], refs[count], refs[-1]

        @pl.when(pl.program_id(0) == 0)
        def _():
            for q in range(2):
                x = jnp.exp(s[q] - log_sum(mine_ref[q], got_ref[1 - q]))
                if 0 in group and q == 0:
                    lane = lax.broadcasted_iota(jnp.int32, x.shape, 1)
                    local = sum(places[0]) - PASSAGES
                    x = x - (lane == pos[...] + local).astype(jnp.float32)
                w[q] = x.astype(jnp.bfloat16)
                if n % 128:
                    x = jnp.concatenate([x, jnp.zeros((rows, 128 - n % 128), jnp.float32)], 1)
                turned[q] = x.T[:n].astype(jnp.bfloat16)

        for q, ref in enumerate((own, oth)):
            g = jnp.dot(turned[q], ref[...], preferred_element_type=jnp.float32)
            for k, (ch, m) in enumerate(zip(group, sizes)):
                at = places[ch][0]
                for r in range(4):
                    outs[4 * k + r][q] = g[at : at + m].astype(jnp.bfloat16)
                    at += m
                if ch == 0 and q == 0:
                    refs[count + 1][...] = g[at : at + PASSAGES]

    query = pl.BlockSpec((rows, tile), lambda i: (0, i))
    stat = pl.BlockSpec((2, rows, 128), lambda i: (0, 0, 0))
    outs = [m for m in sizes for _ in range(4)]
    out_shape = [bf16(2, m, WIDTH) for m in outs] + [bf16(2, rows, n)]
    out_specs = [pl.BlockSpec((2, m, tile), lambda i: (0, 0, i)) for m in outs]
    out_specs.append(pl.BlockSpec((2, rows, n), lambda i: (0, 0, 0)))
    if 0 in group:
        out_shape.append(jax.ShapeDtypeStruct((PASSAGES, WIDTH), jnp.float32))
        out_specs.append(pl.BlockSpec((PASSAGES, tile), lambda i: (0, i)))
    return pl.pallas_call(
        body,
        grid=(4,),
        out_shape=out_shape,
        in_specs=[
            pl.BlockSpec((2, rows, n), lambda i: (0, 0, column // n)),
            stat,
            stat,
            query,
            query,
            pl.BlockSpec((rows, 1), lambda i: (0, 0)),
        ],
        out_specs=out_specs,
        scratch_shapes=[pltpu.VMEM((2, n, rows), jnp.bfloat16)],
        compiler_params=pltpu.CompilerParams(vmem_limit_bytes=56 * 2**20),
        cost_estimate=pl.CostEstimate(flops=0, bytes_accessed=COST, transcendentals=0),
    )(scores, mine, got, queries, others, positive)


def query_sums(q, weights, keys, more=None):
    rows = weights[0].shape[1]
    tile = WIDTH // 4
    widths = [w.shape[2] for w in weights]

    def body(*refs):
        w_refs, parts = refs[: len(weights)], refs[len(weights) : len(weights) + len(keys)]
        out, w_all, held = refs[-3:]

        @pl.when(pl.program_id(0) == 0)
        def _():
            at = 0
            for w, n in zip(w_refs, widths):
                w_all[:, at : at + n] = w[0]
                at += n

        at = 0
        for ref in parts:
            m = ref.shape[1]
            held[at : at + m, :] = ref[0]
            at += m
        total = jnp.dot(w_all[...], held[...], preferred_element_type=jnp.float32)
        if more is not None:
            total = total + refs[len(weights) + len(keys)][...].astype(jnp.float32)
        out[...] = total.astype(out.dtype)

    specs = [pl.BlockSpec((1, rows, n), lambda i: (q, 0, 0)) for n in widths]
    for k in keys:
        last = k.shape[0] - 1
        specs.append(pl.BlockSpec((1, k.shape[1], tile), lambda i, at=min(q, last): (at, 0, i)))
    args = [*weights, *keys]
    if more is not None:
        args.append(more)
        specs.append(pl.BlockSpec((rows, tile), lambda i: (0, i)))
    return pl.pallas_call(
        body,
        grid=(4,),
        out_shape=bf16(rows, WIDTH),
        in_specs=specs,
        out_specs=pl.BlockSpec((rows, tile), lambda i: (0, i)),
        scratch_shapes=[
            pltpu.VMEM((rows, sum(widths)), jnp.bfloat16),
            pltpu.VMEM((sum(widths), tile), jnp.bfloat16),
        ],
        compiler_params=pltpu.CompilerParams(vmem_limit_bytes=56 * 2**20),
        cost_estimate=pl.CostEstimate(flops=0, bytes_accessed=COST, transcendentals=0),
    )(*args)


def add_up(table, parts):
    counts = [len(ring) for *_, ring in parts]
    tile = WIDTH // 2

    def body(tab, *refs):
        n = len(parts)
        outs, accs = refs[-2 * n : -n], refs[-n:]
        pos = 0
        for (iz, *_), count, out, acc in zip(parts, counts, outs, accs):
            row = refs[pos : pos + 4]
            ring = refs[pos + 4 : pos + 4 + count]
            pos += 4 + count
            if ring:
                total = ring[0][...].astype(jnp.float32)
                for r in ring[1:]:
                    total = total + r[...].astype(jnp.float32)
                acc[...] = total
            else:
                acc[...] = jnp.zeros_like(acc)
            for t in range(4):
                for q in range(2):
                    for p in range(CAP):
                        at = pick(tab, TO[t], q, 0, DZ[iz], p)
                        acc[at] += row[t][q, 0, p].astype(jnp.float32)
            out[...] = acc[...].astype(out.dtype)

    whole = pl.BlockSpec((BLOCKS, BR, tile), lambda n: (0, 0, n))
    args, specs = [], []
    for iz, j, row, ring in parts:
        args += [*row, *ring]
        specs += [pl.BlockSpec((2, 1, CAP, BR, tile), lambda n, j=j: (0, j, 0, 0, n))] * 4
        specs += [whole] * len(ring)
    return pl.pallas_call(
        body,
        grid=(2,),
        out_shape=[bf16(BLOCKS, BR, WIDTH)] * len(parts),
        in_specs=[SMEM] + specs,
        out_specs=[whole] * len(parts),
        scratch_shapes=[pltpu.VMEM((BLOCKS, BR, tile), jnp.float32)] * len(parts),
        compiler_params=pltpu.CompilerParams(vmem_limit_bytes=32 * 2**20),
        cost_estimate=pl.CostEstimate(flops=0, bytes_accessed=COST, transcendentals=0),
    )(table, *args)


def total_of(term):
    total = jnp.full((1, 128), term)
    for step in (1, 2):
        total = total + lax.ppermute(total, "group", [(i, i ^ step) for i in range(4)])
    total = jnp.broadcast_to(total, (NX * NZ * NC, 128))
    return jnp.sum(lax.all_to_all(total, "member", 0, 0, tiled=True)[:, 0])


def after(x, *earlier):
    if not earlier:
        return x
    return lax.optimization_barrier((x, earlier))[0]


def tables(pair_blocks):
    me = lax.axis_index("member")
    grp = lax.axis_index("group")
    x, z, c = me // (NZ * NC), (me // NC) % NZ, me % NC
    size = NX * NZ * NC
    rows = [
        lax.dynamic_slice(
            pair_blocks,
            (grp * size + member(x + d, z, 0), 0, 0),
            (NC, size - 1, CAP),
        )
        for d in range(NX)
    ]
    rows = jnp.concatenate(rows).reshape(-1)
    return jnp.concatenate([rows, jnp.stack([x, z, c]).astype(jnp.int32)])


def shards(queries, passages, pair_blocks, positive):
    rows_q = queries.shape[0]
    positive = positive.reshape(rows_q, 1)
    blocks = passages.reshape(BLOCKS, BR, WIDTH)

    a = {0: blocks, 1: hop(blocks, dz=-1), -1: hop(blocks, dz=1)}
    table = tables(pair_blocks)
    keys = []
    for k, chunk in enumerate(CHUNKS):
        if k > 1:
            gate = (*keys[0][1:], *sent) if k == 2 else (others,) if k == 3 else ()
            if k < 4:
                a[k] = hop(after(a[k - 1], *gate), dz=-1)
            a[-k if k < 4 else 4] = hop(after(a[-k + 1], *gate), dz=1)
        pieces = [a[DZ[iz]] for iz in chunk]
        if k == 1:
            pieces = after(pieces, *sent)
        mine, *sent = pack(table, chunk, pieces)
        going = after(sent, *keys[k - 2][1:]) if k > 1 else sent
        if k == 4:
            flat_keys = [[flat(part) for part in key] for key in keys]
            early, own = score(LOOKS[0], flat_keys, queries, others, passages, positive, None)
            going = after(going, own)
        keys.append([mine] + [hop(s, dx=t) for s, t in zip(going, TO[1:])])
        if k == 1:
            others = hop(after(queries, *keys[0][1:], *sent), dc=1)
    flat_keys.append([flat(part) for part in keys[4]])
    late, own = score(LOOKS[1], flat_keys, queries, others, passages, positive, own)
    got = hop(own, dc=1)

    grads, weights, come = {}, {}, {}

    def products(group, scores, column=0):
        made = partials(group, scores, column, own, got, queries, others, positive)
        for k, ch in enumerate(group):
            n = len(CHUNKS[ch])
            grads[ch] = [g.reshape(2, n, CAP, BR, WIDTH) for g in made[4 * k : 4 * k + 4]]
        weights[group] = made[4 * len(group)]
        return made[-1]

    def send(ch, *earlier):
        to = grads[ch][1:]
        if earlier:
            to = after(to, *earlier)
        come[ch] = [hop(to[1], dx=1), hop(to[0], dx=-1), hop(to[2], dx=2)]

    def row(ch):
        return [grads[ch][0], come[ch][1], come[ch][0], come[ch][2]]

    products(BACK[0], late)
    send(4)
    send(3)
    own_grad = products(BACK[1], after(early, *come[4])).reshape(BLOCKS, BR, WIDTH)
    send(2)
    send(1, *come[3])
    send(0, *come[2])
    (four,) = add_up(table, [(7, 0, row(4), [])])
    up_ring, down_ring = [hop(four, dz=1)], []
    all_keys = [*flat_keys[1], *flat_keys[0], passages[None], *flat_keys[2], *flat_keys[3], *flat_keys[4]]
    all_weights = [weights[group] for group in BACK[::-1]]
    term = jnp.sum(log_sum(own[0], got[1]) - own[0, :, 2:3])
    loss = total_of(after(term, *come[3])) / (rows_q * NX * NZ * NC * 4)
    for ch in (3, 2, 1):
        j, i = CHUNKS[ch]
        rows = row(ch)
        if ch == 2:
            for_other = query_sums(1, after(all_weights, *come[3], up, down), all_keys)
            rows = after(rows, for_other)
        if ch == 1:
            from_other = hop(after(for_other, *come[1], *up_ring, *down_ring, loss), dc=1)
        up, down = add_up(table, [(i, 1, rows, up_ring), (j, 0, rows, down_ring)])
        up_ring, down_ring = [hop(up, dz=1)], [hop(down, dz=-1)]
    query_grad = query_sums(0, all_weights, all_keys, from_other)
    last = after(own_grad, query_grad)
    (passage_grad,) = add_up(table, [(0, 0, row(0), up_ring + down_ring + [last])])
    return (loss, query_grad, passage_grad.reshape(PASSAGES, WIDTH))


def solution(mesh):
    in_specs = (
        P(("group", "member"), None),
        P(("group", "member"), None),
        P(),
        P(("group", "member")),
    )
    out_specs = (P(), P(("group", "member"), None), P(("group", "member"), None))
    return jax.shard_map(shards, mesh=mesh, in_specs=in_specs, out_specs=out_specs, check_vma=False)
```

```python
import jax
import jax.numpy as jnp
from jax import lax
from jax.experimental import pallas as pl
from jax.experimental.pallas import tpu as pltpu
from jax.sharding import PartitionSpec as P

BLOCKS = 8
BR = 8
CAP = 2
NX, NZ, NC = 4, 8, 2
WIDTH = 4096
COST = 1024
PASSAGES = BLOCKS * BR
score_scale = 0.046875

DZ = (0, -1, 1, -2, 2, -3, 3, 4)
TO = (0, 1, -1, 2)
CHUNKS = ((0,), (1, 2), (3, 4), (5, 6), (7,))
LOOKS = ((1, 0, 2), (3, 4))
BACK = ((3, 4), (1, 0, 2))

ANY = pl.BlockSpec(memory_space=pl.ANY)
VMEM = pl.BlockSpec(memory_space=pltpu.VMEM)
SMEM = pl.BlockSpec(memory_space=pltpu.SMEM)


def member(x, z, c):
    return ((x % NX) * NZ + z % NZ) * NC + c % NC


def hop(a, dx=0, dz=0, dc=0):
    pairs = [
        (member(x, z, c), member(x + dx, z + dz, c + dc))
        for x in range(NX)
        for z in range(NZ)
        for c in range(NC)
    ]
    return lax.ppermute(a, "member", pairs)


def pick(tab, d, q, dx, dz, p):
    last = NX * NZ * NC - 2
    base = NX * NC * (last + 1) * CAP
    x, z, c = tab[base], tab[base + 1], tab[base + 2]
    core = c if q == 0 else 1 - c
    query = (((x + d) & (NX - 1)) * NZ + z) * NC + core
    source = (((x + dx) & (NX - 1)) * NZ + ((z + dz) & (NZ - 1))) * NC + c
    offset = jnp.minimum((source - query - 1) & (last + 1), last)
    return tab[(((d % NX) * NC + core) * (last + 1) + offset) * CAP + p]


def bf16(*shape):
    return jax.ShapeDtypeStruct(shape, jnp.bfloat16)


def pack(table, chunk, held):
    n = len(chunk)
    todo = [(t, j, q, p) for t in range(4) for j in range(n) for q in range(2) for p in range(CAP)]

    def body(tab, *refs):
        src, dst, sem = refs[:n], refs[n : n + 4], refs[-1]
        ops = []
        for k, (t, j, q, p) in enumerate(todo):
            at = pick(tab, TO[t], q, 0, DZ[chunk[j]], p)
            ops.append(pltpu.make_async_copy(src[j].at[at], dst[t].at[q, j, p], sem.at[k]))
            ops[-1].start()
        for op in ops:
            op.wait()

    return pl.pallas_call(
        body,
        out_shape=[bf16(2, n, CAP, BR, WIDTH)] * 4,
        in_specs=[SMEM] + [ANY] * n,
        out_specs=[VMEM] * 4,
        scratch_shapes=[pltpu.SemaphoreType.DMA((len(todo),))],
        compiler_params=pltpu.CompilerParams(vmem_limit_bytes=32 * 2**20),
        cost_estimate=pl.CostEstimate(flops=0, bytes_accessed=COST, transcendentals=0),
    )(table, *held)


def flat(part):
    return part.reshape(2, -1, WIDTH)


def columns_of(group):
    at, places = 0, {}
    for ch in group:
        n = 4 * len(CHUNKS[ch]) * CAP * BR + (PASSAGES if ch == 0 else 0)
        places[ch] = (at, n)
        at += n
    return places, -(-at // 128) * 128


def score(group, keys, queries, others, passages, positive, before):
    rows = queries.shape[0]
    tile = rows // 2
    places, n = columns_of(group)
    count = 4 * len(group)
    used = sum(places[group[-1]])

    def body(*refs):
        own, oth = refs[count : count + 2]
        more = refs[count + 2 : -3]
        out, stat, held = refs[-3:]

        @pl.when(pl.program_id(1) == 0)
        def _():
            for k, ch in enumerate(group):
                at, size = places[ch]
                for ref in refs[4 * k : 4 * k + 4]:
                    held[at : at + ref.shape[1], :] = ref[0]
                    at += ref.shape[1]
                if ch == 0:
                    held[at : at + PASSAGES, :] = more[0][...]
            if used < n:
                held[used:, :] = jnp.zeros((n - used, WIDTH), jnp.bfloat16)

        lane = lax.broadcasted_iota(jnp.int32, (tile, n), 1)
        lane_out = lax.broadcasted_iota(jnp.int32, (tile, 128), 1)

        def product(ref, q):
            x = score_scale * lax.dot_general(
                ref[...], held[...], (((1,), (1,)), ((), ())), preferred_element_type=jnp.float32
            )
            if 0 in group:
                start, size = places[0]
                local = start + size - PASSAGES
                low, high = (start, start + CAP * BR) if q == 0 else (local, start + size)
                x = jnp.where((lane >= low) & (lane < high), -jnp.inf, x)
            if used < n:
                x = jnp.where(lane < used, x, -jnp.inf)
            out[0] = x
            top = jnp.max(x, axis=1, keepdims=True)
            positive_score = jnp.zeros_like(top)
            if before is not None:
                last = more[-1][0]
                rest, top = top, jnp.maximum(top, last[:, 0:1])
                positive_score = last[:, 2:3]
            total = jnp.sum(jnp.exp(x - top), axis=1, keepdims=True)
            if before is not None:
                total = total + last[:, 1:2] * jnp.exp(last[:, 0:1] - top)
            if 0 in group and q == 0:
                hit = lane == more[1][...] + local
                positive_score += jnp.sum(jnp.where(hit, x, 0.0), axis=1, keepdims=True)
            stat[0] = jnp.where(lane_out == 0, top, jnp.where(lane_out == 1, total, positive_score))

        @pl.when(pl.program_id(0) == 0)
        def _():
            product(own, 0)

        @pl.when(pl.program_id(0) == 1)
        def _():
            product(oth, 1)

    args, specs = [], []
    for ch in group:
        for part in keys[ch]:
            args.append(part)
            specs.append(pl.BlockSpec((1, part.shape[1], WIDTH), lambda q, t: (q, 0, 0)))
    args += [queries, others]
    specs += [
        pl.BlockSpec((tile, WIDTH), lambda q, t: (jnp.where(q == 0, t, 1), 0)),
        pl.BlockSpec((tile, WIDTH), lambda q, t: (jnp.where(q == 0, 0, t), 0)),
    ]
    if 0 in group:
        args += [passages, positive]
        specs.append(pl.BlockSpec((PASSAGES, WIDTH), lambda q, t: (0, 0)))
        specs.append(pl.BlockSpec((tile, 1), lambda q, t: (t, 0)))
    if before is not None:
        args.append(before)
        specs.append(pl.BlockSpec((1, tile, 128), lambda q, t: (q, t, 0)))
    return pl.pallas_call(
        body,
        grid=(2, 2),
        out_shape=[
            jax.ShapeDtypeStruct((2, rows, n), jnp.float32),
            jax.ShapeDtypeStruct((2, rows, 128), jnp.float32),
        ],
        in_specs=specs,
        out_specs=[
            pl.BlockSpec((1, tile, n), lambda q, t: (q, t, 0)),
            pl.BlockSpec((1, tile, 128), lambda q, t: (q, t, 0)),
        ],
        scratch_shapes=[pltpu.VMEM((n, WIDTH), jnp.bfloat16)],
        compiler_params=pltpu.CompilerParams(vmem_limit_bytes=56 * 2**20),
        cost_estimate=pl.CostEstimate(flops=0, bytes_accessed=COST, transcendentals=0),
    )(*args)


def log_sum(a, b):
    top = jnp.maximum(a[:, 0:1], b[:, 0:1])
    return top + jnp.log(
        a[:, 1:2] * jnp.exp(a[:, 0:1] - top) + b[:, 1:2] * jnp.exp(b[:, 0:1] - top)
    )


def partials(group, scores, column, mine, got, queries, others, positive):
    rows = queries.shape[0]
    tile = WIDTH // 4
    places, n = columns_of(group)
    sizes = [len(CHUNKS[ch]) * CAP * BR for ch in group]
    count = 4 * len(group)

    def body(s, mine_ref, got_ref, own, oth, pos, *refs):
        outs, w, turned = refs[:count], refs[count], refs[-1]

        @pl.when(pl.program_id(0) == 0)
        def _():
            for q in range(2):
                x = jnp.exp(s[q] - log_sum(mine_ref[q], got_ref[1 - q]))
                if 0 in group and q == 0:
                    lane = lax.broadcasted_iota(jnp.int32, x.shape, 1)
                    local = sum(places[0]) - PASSAGES
                    x = x - (lane == pos[...] + local).astype(jnp.float32)
                w[q] = x.astype(jnp.bfloat16)
                turned[q] = x.T.astype(jnp.bfloat16)

        for q, ref in enumerate((own, oth)):
            g = jnp.dot(turned[q], ref[...], preferred_element_type=jnp.float32)
            for k, (ch, m) in enumerate(zip(group, sizes)):
                at = places[ch][0]
                for r in range(4):
                    outs[4 * k + r][q] = g[at : at + m].astype(jnp.bfloat16)
                    at += m
                if ch == 0 and q == 0:
                    refs[count + 1][...] = g[at : at + PASSAGES]

    query = pl.BlockSpec((rows, tile), lambda i: (0, i))
    stat = pl.BlockSpec((2, rows, 128), lambda i: (0, 0, 0))
    outs = [m for m in sizes for _ in range(4)]
    out_shape = [bf16(2, m, WIDTH) for m in outs] + [bf16(2, rows, n)]
    out_specs = [pl.BlockSpec((2, m, tile), lambda i: (0, 0, i)) for m in outs]
    out_specs.append(pl.BlockSpec((2, rows, n), lambda i: (0, 0, 0)))
    if 0 in group:
        out_shape.append(jax.ShapeDtypeStruct((PASSAGES, WIDTH), jnp.float32))
        out_specs.append(pl.BlockSpec((PASSAGES, tile), lambda i: (0, i)))
    return pl.pallas_call(
        body,
        grid=(4,),
        out_shape=out_shape,
        in_specs=[
            pl.BlockSpec((2, rows, n), lambda i: (0, 0, column // n)),
            stat,
            stat,
            query,
            query,
            pl.BlockSpec((rows, 1), lambda i: (0, 0)),
        ],
        out_specs=out_specs,
        scratch_shapes=[pltpu.VMEM((2, n, rows), jnp.bfloat16)],
        compiler_params=pltpu.CompilerParams(vmem_limit_bytes=56 * 2**20),
        cost_estimate=pl.CostEstimate(flops=0, bytes_accessed=COST, transcendentals=0),
    )(scores, mine, got, queries, others, positive)


def query_sums(q, weights, keys, more=None):
    rows = weights[0].shape[1]
    tile = WIDTH // 2
    widths = [w.shape[2] for w in weights]

    def body(*refs):
        w_refs, parts = refs[: len(weights)], refs[len(weights) : len(weights) + len(keys)]
        out, w_all, held = refs[-3:]

        @pl.when(pl.program_id(0) == 0)
        def _():
            at = 0
            for w, n in zip(w_refs, widths):
                w_all[:, at : at + n] = w[0]
                at += n

        at = 0
        for ref in parts:
            m = ref.shape[1]
            held[at : at + m, :] = ref[0]
            at += m
        if at < sum(widths):
            held[at:, :] = jnp.zeros((sum(widths) - at, tile), jnp.bfloat16)
        total = jnp.dot(w_all[...], held[...], preferred_element_type=jnp.float32)
        if more is not None:
            total = total + refs[len(weights) + len(keys)][...].astype(jnp.float32)
        out[...] = total.astype(out.dtype)

    specs = [pl.BlockSpec((1, rows, n), lambda i: (q, 0, 0)) for n in widths]
    for k in keys:
        last = k.shape[0] - 1
        specs.append(pl.BlockSpec((1, k.shape[1], tile), lambda i, at=min(q, last): (at, 0, i)))
    args = [*weights, *keys]
    if more is not None:
        args.append(more)
        specs.append(pl.BlockSpec((rows, tile), lambda i: (0, i)))
    return pl.pallas_call(
        body,
        grid=(2,),
        out_shape=bf16(rows, WIDTH),
        in_specs=specs,
        out_specs=pl.BlockSpec((rows, tile), lambda i: (0, i)),
        scratch_shapes=[
            pltpu.VMEM((rows, sum(widths)), jnp.bfloat16),
            pltpu.VMEM((sum(widths), tile), jnp.bfloat16),
        ],
        compiler_params=pltpu.CompilerParams(vmem_limit_bytes=56 * 2**20),
        cost_estimate=pl.CostEstimate(flops=0, bytes_accessed=COST, transcendentals=0),
    )(*args)


def add_up(table, parts):
    counts = [len(ring) for *_, ring in parts]
    tile = WIDTH // 2

    def body(tab, *refs):
        n = len(parts)
        outs, accs = refs[-2 * n : -n], refs[-n:]
        pos = 0
        for (iz, *_), count, out, acc in zip(parts, counts, outs, accs):
            row = refs[pos : pos + 4]
            ring = refs[pos + 4 : pos + 4 + count]
            pos += 4 + count
            if ring:
                total = ring[0][...].astype(jnp.float32)
                for r in ring[1:]:
                    total = total + r[...].astype(jnp.float32)
                acc[...] = total
            else:
                acc[...] = jnp.zeros_like(acc)
            for t in range(4):
                for q in range(2):
                    for p in range(CAP):
                        at = pick(tab, TO[t], q, 0, DZ[iz], p)
                        acc[at] += row[t][q, 0, p].astype(jnp.float32)
            out[...] = acc[...].astype(out.dtype)

    whole = pl.BlockSpec((BLOCKS, BR, tile), lambda n: (0, 0, n))
    args, specs = [], []
    for iz, j, row, ring in parts:
        args += [*row, *ring]
        specs += [pl.BlockSpec((2, 1, CAP, BR, tile), lambda n, j=j: (0, j, 0, 0, n))] * 4
        specs += [whole] * len(ring)
    return pl.pallas_call(
        body,
        grid=(2,),
        out_shape=[bf16(BLOCKS, BR, WIDTH)] * len(parts),
        in_specs=[SMEM] + specs,
        out_specs=[whole] * len(parts),
        scratch_shapes=[pltpu.VMEM((BLOCKS, BR, tile), jnp.float32)] * len(parts),
        compiler_params=pltpu.CompilerParams(vmem_limit_bytes=32 * 2**20),
        cost_estimate=pl.CostEstimate(flops=0, bytes_accessed=COST, transcendentals=0),
    )(table, *args)


def sum_groups(term):
    total = jnp.full((1, 128), term)
    for step in (1, 2):
        total = total + lax.ppermute(total, "group", [(i, i ^ step) for i in range(4)])
    return total


def sum_members(total):
    total = jnp.broadcast_to(total, (NX * NZ * NC, 128))
    return jnp.sum(lax.all_to_all(total, "member", 0, 0, tiled=True)[:, 0])


def after(x, *earlier):
    if not earlier:
        return x
    return lax.optimization_barrier((x, earlier))[0]


def tables(pair_blocks):
    me = lax.axis_index("member")
    grp = lax.axis_index("group")
    x, z, c = me // (NZ * NC), (me // NC) % NZ, me % NC
    size = NX * NZ * NC
    rows = [
        lax.dynamic_slice(
            pair_blocks,
            (grp * size + member(x + d, z, 0), 0, 0),
            (NC, size - 1, CAP),
        )
        for d in range(NX)
    ]
    rows = jnp.concatenate(rows).reshape(-1)
    return jnp.concatenate([rows, jnp.stack([x, z, c]).astype(jnp.int32)])


def shards(queries, passages, pair_blocks, positive):
    rows_q = queries.shape[0]
    positive = positive.reshape(rows_q, 1)
    blocks = passages.reshape(BLOCKS, BR, WIDTH)

    a = {0: blocks, 1: hop(blocks, dz=-1), -1: hop(blocks, dz=1)}
    table = tables(pair_blocks)
    keys = []
    for k, chunk in enumerate(CHUNKS):
        if k > 1:
            gate = (*keys[0][1:], *sent) if k == 2 else (others,) if k == 3 else ()
            if k < 4:
                a[k] = hop(after(a[k - 1], *gate), dz=-1)
            a[-k if k < 4 else 4] = hop(after(a[-k + 1], *gate), dz=1)
        pieces = [a[DZ[iz]] for iz in chunk]
        if k == 1:
            pieces = after(pieces, *sent)
        mine, *sent = pack(table, chunk, pieces)
        going = after(sent, *keys[k - 2][1:]) if k > 1 else sent
        if k == 4:
            flat_keys = [[flat(part) for part in key] for key in keys]
            early, own = score(LOOKS[0], flat_keys, queries, others, passages, positive, None)
            going = after(going, own)
        keys.append([mine] + [hop(s, dx=t) for s, t in zip(going, TO[1:])])
        if k == 1:
            others = hop(after(queries, *keys[0][1:], *sent), dc=1)
    flat_keys.append([flat(part) for part in keys[4]])
    late, own = score(LOOKS[1], flat_keys, queries, others, passages, positive, own)
    got = hop(own, dc=1)

    grads, weights, come = {}, {}, {}

    def products(group, scores, column=0):
        made = partials(group, scores, column, own, got, queries, others, positive)
        for k, ch in enumerate(group):
            n = len(CHUNKS[ch])
            grads[ch] = [g.reshape(2, n, CAP, BR, WIDTH) for g in made[4 * k : 4 * k + 4]]
        weights[group] = made[4 * len(group)]
        return made[-1]

    def send(ch, *earlier):
        to = grads[ch][1:]
        if earlier:
            to = after(to, *earlier)
        come[ch] = [hop(to[1], dx=1), hop(to[0], dx=-1), hop(to[2], dx=2)]

    def row(ch):
        return [grads[ch][0], come[ch][1], come[ch][0], come[ch][2]]

    products(BACK[0], late)
    send(4)
    send(3)
    mine, other = after((own[0], got[1]), weights[BACK[0]])
    term = sum_groups(jnp.sum(log_sum(mine, other) - mine[:, 2:3]))
    own_grad = products(BACK[1], after(early, *come[4])).reshape(BLOCKS, BR, WIDTH)
    send(2)
    send(1, *come[3])
    send(0, *come[2])
    (four,) = add_up(table, [(7, 0, after(row(4), term), [])])
    up_ring, down_ring = [hop(four, dz=1)], []
    all_keys = [*flat_keys[1], *flat_keys[0], passages[None], *flat_keys[2], *flat_keys[3], *flat_keys[4]]
    all_weights = [weights[group] for group in BACK[::-1]]
    loss = sum_members(after(term, *come[2])) / (rows_q * NX * NZ * NC * 4)
    for ch in (3, 2, 1):
        j, i = CHUNKS[ch]
        rows = row(ch)
        if ch == 2:
            for_other = query_sums(1, after(all_weights, *come[3], up, down), all_keys)
            rows = after(rows, for_other)
        if ch == 1:
            from_other = hop(after(for_other, *come[1], *up_ring, *down_ring, loss), dc=1)
        up, down = add_up(table, [(i, 1, rows, up_ring), (j, 0, rows, down_ring)])
        up_ring, down_ring = [hop(up, dz=1)], [hop(down, dz=-1)]
    query_grad = query_sums(0, all_weights, all_keys, from_other)
    last = after(own_grad, query_grad)
    (passage_grad,) = add_up(table, [(0, 0, row(0), up_ring + down_ring + [last])])
    return (loss, query_grad, passage_grad.reshape(PASSAGES, WIDTH))


def solution(mesh):
    in_specs = (
        P(("group", "member"), None),
        P(("group", "member"), None),
        P(),
        P(("group", "member")),
    )
    out_specs = (P(), P(("group", "member"), None), P(("group", "member"), None))
    return jax.shard_map(shards, mesh=mesh, in_specs=in_specs, out_specs=out_specs, check_vma=False)
```

```python
import jax
import jax.numpy as jnp
from jax import lax
from jax.experimental import pallas as pl
from jax.experimental.pallas import tpu as pltpu
from jax.sharding import PartitionSpec as P

BLOCKS = 8
BR = 8
CAP = 2
NX, NZ, NC = 4, 8, 2
WIDTH = 4096
COST = 1024
PASSAGES = BLOCKS * BR
score_scale = 0.046875

DZ = (0, -1, 1, -2, 2, -3, 3, 4)
TO = (0, 1, -1, 2)
CHUNKS = ((0,), (1, 2), (3, 4), (5, 6), (7,))
LOOKS = ((1, 0, 2), (3, 4))
BACK = ((3, 4), (1, 0, 2))

ANY = pl.BlockSpec(memory_space=pl.ANY)
VMEM = pl.BlockSpec(memory_space=pltpu.VMEM)
SMEM = pl.BlockSpec(memory_space=pltpu.SMEM)


def member(x, z, c):
    return ((x % NX) * NZ + z % NZ) * NC + c % NC


def hop(a, dx=0, dz=0, dc=0):
    pairs = [
        (member(x, z, c), member(x + dx, z + dz, c + dc))
        for x in range(NX)
        for z in range(NZ)
        for c in range(NC)
    ]
    return lax.ppermute(a, "member", pairs)


def pick(tab, d, q, dx, dz, p):
    last = NX * NZ * NC - 2
    base = NX * NC * (last + 1) * CAP
    x, z, c = tab[base], tab[base + 1], tab[base + 2]
    core = c if q == 0 else 1 - c
    query = (((x + d) & (NX - 1)) * NZ + z) * NC + core
    source = (((x + dx) & (NX - 1)) * NZ + ((z + dz) & (NZ - 1))) * NC + c
    offset = jnp.minimum((source - query - 1) & (last + 1), last)
    return tab[(((d % NX) * NC + core) * (last + 1) + offset) * CAP + p]


def bf16(*shape):
    return jax.ShapeDtypeStruct(shape, jnp.bfloat16)


def pack(table, chunk, held):
    n = len(chunk)
    todo = [(t, j, q, p) for t in range(4) for j in range(n) for q in range(2) for p in range(CAP)]

    def body(tab, *refs):
        src, dst, sem = refs[:n], refs[n : n + 4], refs[-1]
        ops = []
        for k, (t, j, q, p) in enumerate(todo):
            at = pick(tab, TO[t], q, 0, DZ[chunk[j]], p)
            ops.append(pltpu.make_async_copy(src[j].at[at], dst[t].at[q, j, p], sem.at[k]))
            ops[-1].start()
        for op in ops:
            op.wait()

    return pl.pallas_call(
        body,
        out_shape=[bf16(2, n, CAP, BR, WIDTH)] * 4,
        in_specs=[SMEM] + [ANY] * n,
        out_specs=[VMEM] * 4,
        scratch_shapes=[pltpu.SemaphoreType.DMA((len(todo),))],
        compiler_params=pltpu.CompilerParams(vmem_limit_bytes=32 * 2**20),
        cost_estimate=pl.CostEstimate(flops=0, bytes_accessed=COST, transcendentals=0),
    )(table, *held)


def flat(part):
    return part.reshape(2, -1, WIDTH)


def columns_of(group):
    at, places = 0, {}
    for ch in group:
        n = 4 * len(CHUNKS[ch]) * CAP * BR + (PASSAGES if ch == 0 else 0)
        places[ch] = (at, n)
        at += n
    return places, -(-at // 128) * 128


def score(group, keys, queries, others, passages, positive, before):
    rows = queries.shape[0]
    tile = rows // 2
    places, n = columns_of(group)
    count = 4 * len(group)
    used = sum(places[group[-1]])

    def body(*refs):
        own, oth = refs[count : count + 2]
        more = refs[count + 2 : -3]
        out, stat, held = refs[-3:]

        @pl.when(pl.program_id(1) == 0)
        def _():
            for k, ch in enumerate(group):
                at, size = places[ch]
                for ref in refs[4 * k : 4 * k + 4]:
                    held[at : at + ref.shape[1], :] = ref[0]
                    at += ref.shape[1]
                if ch == 0:
                    held[at : at + PASSAGES, :] = more[0][...]
            if used < n:
                held[used:, :] = jnp.zeros((n - used, WIDTH), jnp.bfloat16)

        lane = lax.broadcasted_iota(jnp.int32, (tile, n), 1)
        lane_out = lax.broadcasted_iota(jnp.int32, (tile, 128), 1)

        def product(ref, q):
            x = score_scale * lax.dot_general(
                ref[...], held[...], (((1,), (1,)), ((), ())), preferred_element_type=jnp.float32
            )
            if 0 in group:
                start, size = places[0]
                local = start + size - PASSAGES
                low, high = (start, start + CAP * BR) if q == 0 else (local, start + size)
                x = jnp.where((lane >= low) & (lane < high), -jnp.inf, x)
            if used < n:
                x = jnp.where(lane < used, x, -jnp.inf)
            out[0] = x
            top = jnp.max(x, axis=1, keepdims=True)
            positive_score = jnp.zeros_like(top)
            if before is not None:
                last = more[-1][0]
                rest, top = top, jnp.maximum(top, last[:, 0:1])
                positive_score = last[:, 2:3]
            total = jnp.sum(jnp.exp(x - top), axis=1, keepdims=True)
            if before is not None:
                total = total + last[:, 1:2] * jnp.exp(last[:, 0:1] - top)
            if 0 in group and q == 0:
                hit = lane == more[1][...] + local
                positive_score += jnp.sum(jnp.where(hit, x, 0.0), axis=1, keepdims=True)
            stat[0] = jnp.where(lane_out == 0, top, jnp.where(lane_out == 1, total, positive_score))

        @pl.when(pl.program_id(0) == 0)
        def _():
            product(own, 0)

        @pl.when(pl.program_id(0) == 1)
        def _():
            product(oth, 1)

    args, specs = [], []
    for ch in group:
        for part in keys[ch]:
            args.append(part)
            specs.append(pl.BlockSpec((1, part.shape[1], WIDTH), lambda q, t: (q, 0, 0)))
    args += [queries, others]
    specs += [
        pl.BlockSpec((tile, WIDTH), lambda q, t: (jnp.where(q == 0, t, 1), 0)),
        pl.BlockSpec((tile, WIDTH), lambda q, t: (jnp.where(q == 0, 0, t), 0)),
    ]
    if 0 in group:
        args += [passages, positive]
        specs.append(pl.BlockSpec((PASSAGES, WIDTH), lambda q, t: (0, 0)))
        specs.append(pl.BlockSpec((tile, 1), lambda q, t: (t, 0)))
    if before is not None:
        args.append(before)
        specs.append(pl.BlockSpec((1, tile, 128), lambda q, t: (q, t, 0)))
    return pl.pallas_call(
        body,
        grid=(2, 2),
        out_shape=[
            jax.ShapeDtypeStruct((2, rows, n), jnp.float32),
            jax.ShapeDtypeStruct((2, rows, 128), jnp.float32),
        ],
        in_specs=specs,
        out_specs=[
            pl.BlockSpec((1, tile, n), lambda q, t: (q, t, 0)),
            pl.BlockSpec((1, tile, 128), lambda q, t: (q, t, 0)),
        ],
        scratch_shapes=[pltpu.VMEM((n, WIDTH), jnp.bfloat16)],
        compiler_params=pltpu.CompilerParams(vmem_limit_bytes=56 * 2**20),
        cost_estimate=pl.CostEstimate(flops=0, bytes_accessed=COST, transcendentals=0),
    )(*args)


def log_sum(a, b):
    top = jnp.maximum(a[:, 0:1], b[:, 0:1])
    return top + jnp.log(
        a[:, 1:2] * jnp.exp(a[:, 0:1] - top) + b[:, 1:2] * jnp.exp(b[:, 0:1] - top)
    )


def partials(group, scores, column, mine, got, queries, others, positive):
    rows = queries.shape[0]
    tile = WIDTH // 4
    places, n = columns_of(group)
    sizes = [len(CHUNKS[ch]) * CAP * BR for ch in group]
    count = 4 * len(group)

    def body(s, mine_ref, got_ref, own, oth, pos, *refs):
        outs, w, turned = refs[:count], refs[count], refs[-1]

        @pl.when(pl.program_id(0) == 0)
        def _():
            for q in range(2):
                x = jnp.exp(s[q] - log_sum(mine_ref[q], got_ref[1 - q]))
                if 0 in group and q == 0:
                    lane = lax.broadcasted_iota(jnp.int32, x.shape, 1)
                    local = sum(places[0]) - PASSAGES
                    x = x - (lane == pos[...] + local).astype(jnp.float32)
                w[q] = x.astype(jnp.bfloat16)
                turned[q] = x.T.astype(jnp.bfloat16)

        for q, ref in enumerate((own, oth)):
            g = jnp.dot(turned[q], ref[...], preferred_element_type=jnp.float32)
            for k, (ch, m) in enumerate(zip(group, sizes)):
                at = places[ch][0]
                for r in range(4):
                    outs[4 * k + r][q] = g[at : at + m].astype(jnp.bfloat16)
                    at += m
                if ch == 0 and q == 0:
                    refs[count + 1][...] = g[at : at + PASSAGES]

    query = pl.BlockSpec((rows, tile), lambda i: (0, i))
    stat = pl.BlockSpec((2, rows, 128), lambda i: (0, 0, 0))
    outs = [m for m in sizes for _ in range(4)]
    out_shape = [bf16(2, m, WIDTH) for m in outs] + [bf16(2, rows, n)]
    out_specs = [pl.BlockSpec((2, m, tile), lambda i: (0, 0, i)) for m in outs]
    out_specs.append(pl.BlockSpec((2, rows, n), lambda i: (0, 0, 0)))
    if 0 in group:
        out_shape.append(jax.ShapeDtypeStruct((PASSAGES, WIDTH), jnp.float32))
        out_specs.append(pl.BlockSpec((PASSAGES, tile), lambda i: (0, i)))
    return pl.pallas_call(
        body,
        grid=(4,),
        out_shape=out_shape,
        in_specs=[
            pl.BlockSpec((2, rows, n), lambda i: (0, 0, column // n)),
            stat,
            stat,
            query,
            query,
            pl.BlockSpec((rows, 1), lambda i: (0, 0)),
        ],
        out_specs=out_specs,
        scratch_shapes=[pltpu.VMEM((2, n, rows), jnp.bfloat16)],
        compiler_params=pltpu.CompilerParams(vmem_limit_bytes=56 * 2**20),
        cost_estimate=pl.CostEstimate(flops=0, bytes_accessed=COST, transcendentals=0),
    )(scores, mine, got, queries, others, positive)


def query_sums(q, weights, keys, more=None):
    rows = weights[0].shape[1]
    tile = WIDTH // 2
    widths = [w.shape[2] for w in weights]

    def body(*refs):
        w_refs, parts = refs[: len(weights)], refs[len(weights) : len(weights) + len(keys)]
        out, w_all, held = refs[-3:]

        @pl.when(pl.program_id(0) == 0)
        def _():
            at = 0
            for w, n in zip(w_refs, widths):
                w_all[:, at : at + n] = w[0]
                at += n

        at = 0
        for ref in parts:
            m = ref.shape[1]
            held[at : at + m, :] = ref[0]
            at += m
        if at < sum(widths):
            held[at:, :] = jnp.zeros((sum(widths) - at, tile), jnp.bfloat16)
        total = jnp.dot(w_all[...], held[...], preferred_element_type=jnp.float32)
        if more is not None:
            total = total + refs[len(weights) + len(keys)][...].astype(jnp.float32)
        out[...] = total.astype(out.dtype)

    specs = [pl.BlockSpec((1, rows, n), lambda i: (q, 0, 0)) for n in widths]
    for k in keys:
        last = k.shape[0] - 1
        specs.append(pl.BlockSpec((1, k.shape[1], tile), lambda i, at=min(q, last): (at, 0, i)))
    args = [*weights, *keys]
    if more is not None:
        args.append(more)
        specs.append(pl.BlockSpec((rows, tile), lambda i: (0, i)))
    return pl.pallas_call(
        body,
        grid=(2,),
        out_shape=bf16(rows, WIDTH),
        in_specs=specs,
        out_specs=pl.BlockSpec((rows, tile), lambda i: (0, i)),
        scratch_shapes=[
            pltpu.VMEM((rows, sum(widths)), jnp.bfloat16),
            pltpu.VMEM((sum(widths), tile), jnp.bfloat16),
        ],
        compiler_params=pltpu.CompilerParams(vmem_limit_bytes=56 * 2**20),
        cost_estimate=pl.CostEstimate(flops=0, bytes_accessed=COST, transcendentals=0),
    )(*args)


def add_up(table, parts):
    counts = [len(ring) for *_, ring in parts]
    tile = WIDTH // 2

    def body(tab, *refs):
        n = len(parts)
        outs, accs = refs[-2 * n : -n], refs[-n:]
        pos = 0
        for (iz, *_), count, out, acc in zip(parts, counts, outs, accs):
            row = refs[pos : pos + 4]
            ring = refs[pos + 4 : pos + 4 + count]
            pos += 4 + count
            if ring:
                total = ring[0][...].astype(jnp.float32)
                for r in ring[1:]:
                    total = total + r[...].astype(jnp.float32)
                acc[...] = total
            else:
                acc[...] = jnp.zeros_like(acc)
            for t in range(4):
                for q in range(2):
                    for p in range(CAP):
                        at = pick(tab, TO[t], q, 0, DZ[iz], p)
                        acc[at] += row[t][q, 0, p].astype(jnp.float32)
            out[...] = acc[...].astype(out.dtype)

    whole = pl.BlockSpec((BLOCKS, BR, tile), lambda n: (0, 0, n))
    args, specs = [], []
    for iz, j, row, ring in parts:
        args += [*row, *ring]
        specs += [pl.BlockSpec((2, 1, CAP, BR, tile), lambda n, j=j: (0, j, 0, 0, n))] * 4
        specs += [whole] * len(ring)
    return pl.pallas_call(
        body,
        grid=(2,),
        out_shape=[bf16(BLOCKS, BR, WIDTH)] * len(parts),
        in_specs=[SMEM] + specs,
        out_specs=[whole] * len(parts),
        scratch_shapes=[pltpu.VMEM((BLOCKS, BR, tile), jnp.float32)] * len(parts),
        compiler_params=pltpu.CompilerParams(vmem_limit_bytes=32 * 2**20),
        cost_estimate=pl.CostEstimate(flops=0, bytes_accessed=COST, transcendentals=0),
    )(table, *args)


def sum_groups(term):
    total = jnp.full((1, 128), term)
    for step in (1, 2):
        total = total + lax.ppermute(total, "group", [(i, i ^ step) for i in range(4)])
    return total


def sum_members(total):
    total = jnp.broadcast_to(total, (NX * NZ * NC, 128))
    return jnp.sum(lax.all_to_all(total, "member", 0, 0, tiled=True)[:, 0])


def after(x, *earlier):
    if not earlier:
        return x
    return lax.optimization_barrier((x, earlier))[0]


def tables(pair_blocks):
    me = lax.axis_index("member")
    grp = lax.axis_index("group")
    x, z, c = me // (NZ * NC), (me // NC) % NZ, me % NC
    size = NX * NZ * NC
    rows = [
        lax.dynamic_slice(
            pair_blocks,
            (grp * size + member(x + d, z, 0), 0, 0),
            (NC, size - 1, CAP),
        )
        for d in range(NX)
    ]
    rows = jnp.concatenate(rows).reshape(-1)
    return jnp.concatenate([rows, jnp.stack([x, z, c]).astype(jnp.int32)])


def shards(queries, passages, pair_blocks, positive):
    rows_q = queries.shape[0]
    positive = positive.reshape(rows_q, 1)
    blocks = passages.reshape(BLOCKS, BR, WIDTH)

    a = {0: blocks, 1: hop(blocks, dz=-1), -1: hop(blocks, dz=1)}
    table = tables(pair_blocks)
    keys = []
    for k, chunk in enumerate(CHUNKS):
        if k > 1:
            gate = (*keys[0][1:], *sent) if k == 2 else (others,) if k == 3 else ()
            if k < 4:
                a[k] = hop(after(a[k - 1], *gate), dz=-1)
            a[-k if k < 4 else 4] = hop(after(a[-k + 1], *gate), dz=1)
        pieces = [a[DZ[iz]] for iz in chunk]
        if k == 1:
            pieces = after(pieces, *sent)
        mine, *sent = pack(table, chunk, pieces)
        going = after(sent, *keys[k - 2][1:]) if k > 1 else sent
        if k == 4:
            flat_keys = [[flat(part) for part in key] for key in keys]
            early, own = score(LOOKS[0], flat_keys, queries, others, passages, positive, None)
            going = after(going, own)
        keys.append([mine] + [hop(s, dx=t) for s, t in zip(going, TO[1:])])
        if k == 1:
            others = hop(after(queries, *keys[0][1:], *sent), dc=1)
    flat_keys.append([flat(part) for part in keys[4]])
    late, own = score(LOOKS[1], flat_keys, queries, others, passages, positive, own)
    got = hop(own, dc=1)

    grads, weights, come = {}, {}, {}

    def products(group, scores, column=0):
        made = partials(group, scores, column, own, got, queries, others, positive)
        for k, ch in enumerate(group):
            n = len(CHUNKS[ch])
            grads[ch] = [g.reshape(2, n, CAP, BR, WIDTH) for g in made[4 * k : 4 * k + 4]]
        weights[group] = made[4 * len(group)]
        return made[-1]

    def send(ch, *earlier):
        to = grads[ch][1:]
        if earlier:
            to = after(to, *earlier)
        come[ch] = [hop(to[1], dx=1), hop(to[0], dx=-1), hop(to[2], dx=2)]

    def row(ch):
        return [grads[ch][0], come[ch][1], come[ch][0], come[ch][2]]

    products(BACK[0], late)
    send(4)
    send(3)
    mine, other = after((own[0], got[1]), *come[4])
    term = sum_groups(jnp.sum(log_sum(mine, other) - mine[:, 2:3]))
    own_grad = products(BACK[1], after(early, *come[4])).reshape(BLOCKS, BR, WIDTH)
    send(2)
    send(1, *come[3])
    send(0, *come[2])
    (four,) = add_up(table, [(7, 0, row(4), [])])
    up_ring, down_ring = [hop(four, dz=1)], []
    all_keys = [*flat_keys[1], *flat_keys[0], passages[None], *flat_keys[2], *flat_keys[3], *flat_keys[4]]
    all_weights = [weights[group] for group in BACK[::-1]]
    loss = sum_members(after(term, *come[2])) / (rows_q * NX * NZ * NC * 4)
    for ch in (3, 2, 1):
        j, i = CHUNKS[ch]
        rows = row(ch)
        if ch == 2:
            for_other = query_sums(1, after(all_weights, *come[3], up, down), all_keys)
            rows = after(rows, for_other, term)
        if ch == 1:
            from_other = hop(after(for_other, *come[1], *up_ring, *down_ring, loss), dc=1)
        up, down = add_up(table, [(i, 1, rows, up_ring), (j, 0, rows, down_ring)])
        up_ring, down_ring = [hop(up, dz=1)], [hop(down, dz=-1)]
    query_grad = query_sums(0, all_weights, all_keys, from_other)
    last = after(own_grad, query_grad)
    (passage_grad,) = add_up(table, [(0, 0, row(0), up_ring + down_ring + [last])])
    return (loss, query_grad, passage_grad.reshape(PASSAGES, WIDTH))


def solution(mesh):
    in_specs = (
        P(("group", "member"), None),
        P(("group", "member"), None),
        P(),
        P(("group", "member")),
    )
    out_specs = (P(), P(("group", "member"), None), P(("group", "member"), None))
    return jax.shard_map(shards, mesh=mesh, in_specs=in_specs, out_specs=out_specs, check_vma=False)
```

```python
import jax
import jax.numpy as jnp
from jax import lax
from jax.experimental import pallas as pl
from jax.experimental.pallas import tpu as pltpu
from jax.sharding import PartitionSpec as P

BLOCKS = 8
BR = 8
CAP = 2
NX, NZ, NC = 4, 8, 2
WIDTH = 4096
COST = 1024
PASSAGES = BLOCKS * BR
score_scale = 0.046875

DZ = (0, -1, 1, -2, 2, -3, 3, 4)
TO = (0, 1, -1, 2)
CHUNKS = ((0,), (1, 2), (3, 4), (5, 6), (7,))
LOOKS = ((1, 0, 2), (3, 4))
BACK = ((3, 4), (1, 0, 2))

ANY = pl.BlockSpec(memory_space=pl.ANY)
VMEM = pl.BlockSpec(memory_space=pltpu.VMEM)
SMEM = pl.BlockSpec(memory_space=pltpu.SMEM)


def member(x, z, c):
    return ((x % NX) * NZ + z % NZ) * NC + c % NC


def hop(a, dx=0, dz=0, dc=0):
    pairs = [
        (member(x, z, c), member(x + dx, z + dz, c + dc))
        for x in range(NX)
        for z in range(NZ)
        for c in range(NC)
    ]
    return lax.ppermute(a, "member", pairs)


def pick(tab, d, q, dx, dz, p):
    last = NX * NZ * NC - 2
    base = NX * NC * (last + 1) * CAP
    x, z, c = tab[base], tab[base + 1], tab[base + 2]
    core = c if q == 0 else 1 - c
    query = (((x + d) & (NX - 1)) * NZ + z) * NC + core
    source = (((x + dx) & (NX - 1)) * NZ + ((z + dz) & (NZ - 1))) * NC + c
    offset = jnp.minimum((source - query - 1) & (last + 1), last)
    return tab[(((d % NX) * NC + core) * (last + 1) + offset) * CAP + p]


def bf16(*shape):
    return jax.ShapeDtypeStruct(shape, jnp.bfloat16)


def pack(table, chunk, held):
    n = len(chunk)
    todo = [(t, j, q, p) for t in range(4) for j in range(n) for q in range(2) for p in range(CAP)]

    def body(tab, *refs):
        src, dst, sem = refs[:n], refs[n : n + 4], refs[-1]
        ops = []
        for k, (t, j, q, p) in enumerate(todo):
            at = pick(tab, TO[t], q, 0, DZ[chunk[j]], p)
            ops.append(pltpu.make_async_copy(src[j].at[at], dst[t].at[q, j, p], sem.at[k]))
            ops[-1].start()
        for op in ops:
            op.wait()

    return pl.pallas_call(
        body,
        out_shape=[bf16(2, n, CAP, BR, WIDTH)] * 4,
        in_specs=[SMEM] + [ANY] * n,
        out_specs=[VMEM] * 4,
        scratch_shapes=[pltpu.SemaphoreType.DMA((len(todo),))],
        compiler_params=pltpu.CompilerParams(vmem_limit_bytes=32 * 2**20),
        cost_estimate=pl.CostEstimate(flops=0, bytes_accessed=COST, transcendentals=0),
    )(table, *held)


def flat(part):
    return part.reshape(2, -1, WIDTH)


def columns_of(group):
    at, places = 0, {}
    for ch in group:
        n = 4 * len(CHUNKS[ch]) * CAP * BR + (PASSAGES if ch == 0 else 0)
        places[ch] = (at, n)
        at += n
    return places, -(-at // 128) * 128


def score(group, keys, queries, others, passages, positive, before):
    rows = queries.shape[0]
    tile = rows // 2
    places, n = columns_of(group)
    count = 4 * len(group)
    used = sum(places[group[-1]])

    def body(*refs):
        own, oth = refs[count : count + 2]
        more = refs[count + 2 : -3]
        out, stat, held = refs[-3:]

        @pl.when(pl.program_id(1) == 0)
        def _():
            for k, ch in enumerate(group):
                at, size = places[ch]
                for ref in refs[4 * k : 4 * k + 4]:
                    held[at : at + ref.shape[1], :] = ref[0]
                    at += ref.shape[1]
                if ch == 0:
                    held[at : at + PASSAGES, :] = more[0][...]
            if used < n:
                held[used:, :] = jnp.zeros((n - used, WIDTH), jnp.bfloat16)

        lane = lax.broadcasted_iota(jnp.int32, (tile, n), 1)
        lane_out = lax.broadcasted_iota(jnp.int32, (tile, 128), 1)

        def product(ref, q):
            x = score_scale * lax.dot_general(
                ref[...], held[...], (((1,), (1,)), ((), ())), preferred_element_type=jnp.float32
            )
            if 0 in group:
                start, size = places[0]
                local = start + size - PASSAGES
                low, high = (start, start + CAP * BR) if q == 0 else (local, start + size)
                x = jnp.where((lane >= low) & (lane < high), -jnp.inf, x)
            if used < n:
                x = jnp.where(lane < used, x, -jnp.inf)
            out[0] = x
            top = jnp.max(x, axis=1, keepdims=True)
            positive_score = jnp.zeros_like(top)
            if before is not None:
                last = more[-1][0]
                rest, top = top, jnp.maximum(top, last[:, 0:1])
                positive_score = last[:, 2:3]
            total = jnp.sum(jnp.exp(x - top), axis=1, keepdims=True)
            if before is not None:
                total = total + last[:, 1:2] * jnp.exp(last[:, 0:1] - top)
            if 0 in group and q == 0:
                hit = lane == more[1][...] + local
                positive_score += jnp.sum(jnp.where(hit, x, 0.0), axis=1, keepdims=True)
            stat[0] = jnp.where(lane_out == 0, top, jnp.where(lane_out == 1, total, positive_score))

        @pl.when(pl.program_id(0) == 0)
        def _():
            product(own, 0)

        @pl.when(pl.program_id(0) == 1)
        def _():
            product(oth, 1)

    args, specs = [], []
    for ch in group:
        for part in keys[ch]:
            args.append(part)
            specs.append(pl.BlockSpec((1, part.shape[1], WIDTH), lambda q, t: (q, 0, 0)))
    args += [queries, others]
    specs += [
        pl.BlockSpec((tile, WIDTH), lambda q, t: (jnp.where(q == 0, t, 1), 0)),
        pl.BlockSpec((tile, WIDTH), lambda q, t: (jnp.where(q == 0, 0, t), 0)),
    ]
    if 0 in group:
        args += [passages, positive]
        specs.append(pl.BlockSpec((PASSAGES, WIDTH), lambda q, t: (0, 0)))
        specs.append(pl.BlockSpec((tile, 1), lambda q, t: (t, 0)))
    if before is not None:
        args.append(before)
        specs.append(pl.BlockSpec((1, tile, 128), lambda q, t: (q, t, 0)))
    return pl.pallas_call(
        body,
        grid=(2, 2),
        out_shape=[
            jax.ShapeDtypeStruct((2, rows, n), jnp.float32),
            jax.ShapeDtypeStruct((2, rows, 128), jnp.float32),
        ],
        in_specs=specs,
        out_specs=[
            pl.BlockSpec((1, tile, n), lambda q, t: (q, t, 0)),
            pl.BlockSpec((1, tile, 128), lambda q, t: (q, t, 0)),
        ],
        scratch_shapes=[pltpu.VMEM((n, WIDTH), jnp.bfloat16)],
        compiler_params=pltpu.CompilerParams(vmem_limit_bytes=56 * 2**20),
        cost_estimate=pl.CostEstimate(flops=0, bytes_accessed=COST, transcendentals=0),
    )(*args)


def log_sum(a, b):
    top = jnp.maximum(a[:, 0:1], b[:, 0:1])
    return top + jnp.log(
        a[:, 1:2] * jnp.exp(a[:, 0:1] - top) + b[:, 1:2] * jnp.exp(b[:, 0:1] - top)
    )


def partials(group, scores, column, mine, got, queries, others, positive):
    rows = queries.shape[0]
    tile = WIDTH // 4
    places, n = columns_of(group)
    sizes = [len(CHUNKS[ch]) * CAP * BR for ch in group]
    count = 4 * len(group)

    def body(s, mine_ref, got_ref, own, oth, pos, *refs):
        outs, w, turned = refs[:count], refs[count], refs[-1]

        @pl.when(pl.program_id(0) == 0)
        def _():
            for q in range(2):
                x = jnp.exp(s[q] - log_sum(mine_ref[q], got_ref[1 - q]))
                if 0 in group and q == 0:
                    lane = lax.broadcasted_iota(jnp.int32, x.shape, 1)
                    local = sum(places[0]) - PASSAGES
                    x = x - (lane == pos[...] + local).astype(jnp.float32)
                w[q] = x.astype(jnp.bfloat16)
                turned[q] = x.T.astype(jnp.bfloat16)

        for q, ref in enumerate((own, oth)):
            g = jnp.dot(turned[q], ref[...], preferred_element_type=jnp.float32)
            for k, (ch, m) in enumerate(zip(group, sizes)):
                at = places[ch][0]
                for r in range(4):
                    outs[4 * k + r][q] = g[at : at + m].astype(jnp.bfloat16)
                    at += m
                if ch == 0 and q == 0:
                    refs[count + 1][...] = g[at : at + PASSAGES]

    query = pl.BlockSpec((rows, tile), lambda i: (0, i))
    stat = pl.BlockSpec((2, rows, 128), lambda i: (0, 0, 0))
    outs = [m for m in sizes for _ in range(4)]
    out_shape = [bf16(2, m, WIDTH) for m in outs] + [bf16(2, rows, n)]
    out_specs = [pl.BlockSpec((2, m, tile), lambda i: (0, 0, i)) for m in outs]
    out_specs.append(pl.BlockSpec((2, rows, n), lambda i: (0, 0, 0)))
    if 0 in group:
        out_shape.append(jax.ShapeDtypeStruct((PASSAGES, WIDTH), jnp.float32))
        out_specs.append(pl.BlockSpec((PASSAGES, tile), lambda i: (0, i)))
    return pl.pallas_call(
        body,
        grid=(4,),
        out_shape=out_shape,
        in_specs=[
            pl.BlockSpec((2, rows, n), lambda i: (0, 0, column // n)),
            stat,
            stat,
            query,
            query,
            pl.BlockSpec((rows, 1), lambda i: (0, 0)),
        ],
        out_specs=out_specs,
        scratch_shapes=[pltpu.VMEM((2, n, rows), jnp.bfloat16)],
        compiler_params=pltpu.CompilerParams(vmem_limit_bytes=56 * 2**20),
        cost_estimate=pl.CostEstimate(flops=0, bytes_accessed=COST, transcendentals=0),
    )(scores, mine, got, queries, others, positive)


def query_sums(q, weights, keys, more=None):
    rows = weights[0].shape[1]
    tile = WIDTH // 2
    widths = [w.shape[2] for w in weights]

    def body(*refs):
        w_refs, parts = refs[: len(weights)], refs[len(weights) : len(weights) + len(keys)]
        out, w_all, held = refs[-3:]

        @pl.when(pl.program_id(0) == 0)
        def _():
            at = 0
            for w, n in zip(w_refs, widths):
                w_all[:, at : at + n] = w[0]
                at += n

        at = 0
        for ref in parts:
            m = ref.shape[1]
            held[at : at + m, :] = ref[0]
            at += m
        if at < sum(widths):
            held[at:, :] = jnp.zeros((sum(widths) - at, tile), jnp.bfloat16)
        total = jnp.dot(w_all[...], held[...], preferred_element_type=jnp.float32)
        if more is not None:
            total = total + refs[len(weights) + len(keys)][...].astype(jnp.float32)
        out[...] = total.astype(out.dtype)

    specs = [pl.BlockSpec((1, rows, n), lambda i: (q, 0, 0)) for n in widths]
    for k in keys:
        last = k.shape[0] - 1
        specs.append(pl.BlockSpec((1, k.shape[1], tile), lambda i, at=min(q, last): (at, 0, i)))
    args = [*weights, *keys]
    if more is not None:
        args.append(more)
        specs.append(pl.BlockSpec((rows, tile), lambda i: (0, i)))
    return pl.pallas_call(
        body,
        grid=(2,),
        out_shape=bf16(rows, WIDTH),
        in_specs=specs,
        out_specs=pl.BlockSpec((rows, tile), lambda i: (0, i)),
        scratch_shapes=[
            pltpu.VMEM((rows, sum(widths)), jnp.bfloat16),
            pltpu.VMEM((sum(widths), tile), jnp.bfloat16),
        ],
        compiler_params=pltpu.CompilerParams(vmem_limit_bytes=56 * 2**20),
        cost_estimate=pl.CostEstimate(flops=0, bytes_accessed=COST, transcendentals=0),
    )(*args)


def add_up(table, parts):
    counts = [len(ring) for *_, ring in parts]
    tile = WIDTH // 2

    def body(tab, *refs):
        n = len(parts)
        outs, accs = refs[-2 * n : -n], refs[-n:]
        pos = 0
        for (iz, *_), count, out, acc in zip(parts, counts, outs, accs):
            row = refs[pos : pos + 4]
            ring = refs[pos + 4 : pos + 4 + count]
            pos += 4 + count
            if ring:
                total = ring[0][...].astype(jnp.float32)
                for r in ring[1:]:
                    total = total + r[...].astype(jnp.float32)
                acc[...] = total
            else:
                acc[...] = jnp.zeros_like(acc)
            for t in range(4):
                for q in range(2):
                    for p in range(CAP):
                        at = pick(tab, TO[t], q, 0, DZ[iz], p)
                        acc[at] += row[t][q, 0, p].astype(jnp.float32)
            out[...] = acc[...].astype(out.dtype)

    whole = pl.BlockSpec((BLOCKS, BR, tile), lambda n: (0, 0, n))
    args, specs = [], []
    for iz, j, row, ring in parts:
        args += [*row, *ring]
        specs += [pl.BlockSpec((2, 1, CAP, BR, tile), lambda n, j=j: (0, j, 0, 0, n))] * 4
        specs += [whole] * len(ring)
    return pl.pallas_call(
        body,
        grid=(2,),
        out_shape=[bf16(BLOCKS, BR, WIDTH)] * len(parts),
        in_specs=[SMEM] + specs,
        out_specs=[whole] * len(parts),
        scratch_shapes=[pltpu.VMEM((BLOCKS, BR, tile), jnp.float32)] * len(parts),
        compiler_params=pltpu.CompilerParams(vmem_limit_bytes=32 * 2**20),
        cost_estimate=pl.CostEstimate(flops=0, bytes_accessed=COST, transcendentals=0),
    )(table, *args)


def sum_groups(term):
    total = jnp.full((1, 128), term)
    for step in (1, 2):
        total = total + lax.ppermute(total, "group", [(i, i ^ step) for i in range(4)])
    return total


def sum_members(total):
    total = jnp.broadcast_to(total, (NX * NZ * NC, 128))
    return jnp.sum(lax.all_to_all(total, "member", 0, 0, tiled=True)[:, 0])


def after(x, *earlier):
    if not earlier:
        return x
    return lax.optimization_barrier((x, earlier))[0]


def tables(pair_blocks):
    me = lax.axis_index("member")
    grp = lax.axis_index("group")
    x, z, c = me // (NZ * NC), (me // NC) % NZ, me % NC
    size = NX * NZ * NC
    rows = [
        lax.dynamic_slice(
            pair_blocks,
            (grp * size + member(x + d, z, 0), 0, 0),
            (NC, size - 1, CAP),
        )
        for d in range(NX)
    ]
    rows = jnp.concatenate(rows).reshape(-1)
    return jnp.concatenate([rows, jnp.stack([x, z, c]).astype(jnp.int32)])


def shards(queries, passages, pair_blocks, positive):
    rows_q = queries.shape[0]
    positive = positive.reshape(rows_q, 1)
    blocks = passages.reshape(BLOCKS, BR, WIDTH)

    a = {0: blocks, 1: hop(blocks, dz=-1), -1: hop(blocks, dz=1)}
    table = tables(pair_blocks)
    keys = []
    for k, chunk in enumerate(CHUNKS):
        if k > 1:
            gate = (*keys[0][1:], *sent) if k == 2 else (others,) if k == 3 else ()
            if k < 4:
                a[k] = hop(after(a[k - 1], *gate), dz=-1)
            a[-k if k < 4 else 4] = hop(after(a[-k + 1], *gate), dz=1)
        pieces = [a[DZ[iz]] for iz in chunk]
        if k == 1:
            pieces = after(pieces, *sent)
        mine, *sent = pack(table, chunk, pieces)
        going = after(sent, *keys[k - 2][1:]) if k > 1 else sent
        if k == 4:
            flat_keys = [[flat(part) for part in key] for key in keys]
            early, own = score(LOOKS[0], flat_keys, queries, others, passages, positive, None)
            going = after(going, own)
        keys.append([mine] + [hop(s, dx=t) for s, t in zip(going, TO[1:])])
        if k == 1:
            others = hop(after(queries, *keys[0][1:], *sent), dc=1)
    flat_keys.append([flat(part) for part in keys[4]])
    late, own = score(LOOKS[1], flat_keys, queries, others, passages, positive, own)
    got = hop(own, dc=1)

    grads, weights, come = {}, {}, {}

    def products(group, scores, column=0):
        made = partials(group, scores, column, own, got, queries, others, positive)
        for k, ch in enumerate(group):
            n = len(CHUNKS[ch])
            grads[ch] = [g.reshape(2, n, CAP, BR, WIDTH) for g in made[4 * k : 4 * k + 4]]
        weights[group] = made[4 * len(group)]
        return made[-1]

    def send(ch, *earlier):
        to = grads[ch][1:]
        if earlier:
            to = after(to, *earlier)
        come[ch] = [hop(to[1], dx=1), hop(to[0], dx=-1), hop(to[2], dx=2)]

    def row(ch):
        return [grads[ch][0], come[ch][1], come[ch][0], come[ch][2]]

    products(BACK[0], late)
    send(4)
    send(3)
    own_grad = products(BACK[1], after(early, *come[4])).reshape(BLOCKS, BR, WIDTH)
    mine, other = after((own[0], got[1]), weights[BACK[1]])
    term = sum_groups(jnp.sum(log_sum(mine, other) - mine[:, 2:3]))
    send(2)
    send(1, *come[3])
    send(0, *come[2])
    (four,) = add_up(table, [(7, 0, row(4), [])])
    up_ring, down_ring = [hop(four, dz=1)], []
    all_keys = [*flat_keys[1], *flat_keys[0], passages[None], *flat_keys[2], *flat_keys[3], *flat_keys[4]]
    all_weights = [weights[group] for group in BACK[::-1]]
    loss = sum_members(after(term, *come[2])) / (rows_q * NX * NZ * NC * 4)
    for ch in (3, 2, 1):
        j, i = CHUNKS[ch]
        rows = row(ch)
        if ch == 2:
            for_other = query_sums(1, after(all_weights, *come[3], up, down), all_keys)
            rows = after(rows, for_other, term)
        if ch == 1:
            from_other = hop(after(for_other, *come[1], *up_ring, *down_ring, loss), dc=1)
        up, down = add_up(table, [(i, 1, rows, up_ring), (j, 0, rows, down_ring)])
        up_ring, down_ring = [hop(up, dz=1)], [hop(down, dz=-1)]
    query_grad = query_sums(0, all_weights, all_keys, from_other)
    last = after(own_grad, query_grad)
    (passage_grad,) = add_up(table, [(0, 0, row(0), up_ring + down_ring + [last])])
    return (loss, query_grad, passage_grad.reshape(PASSAGES, WIDTH))


def solution(mesh):
    in_specs = (
        P(("group", "member"), None),
        P(("group", "member"), None),
        P(),
        P(("group", "member")),
    )
    out_specs = (P(), P(("group", "member"), None), P(("group", "member"), None))
    return jax.shard_map(shards, mesh=mesh, in_specs=in_specs, out_specs=out_specs, check_vma=False)
```
